512 devices in a mesh: tm: 32 (over z, core), space: 16 (over y, x).
Axes of the slice: x: 4, y: 4, z: 16, core: 2. Of those that a mesh axis runs over, the one named last changes fastest.
Arguments:
- blocks: bfloat16 [1536, 48, 48, 128], P(('tm', 'space')), may hold values from -12 to 12
- fields: float32 [1536, 48, 144], P(('tm', 'space')), may hold values from -4 to 4
- trial: bfloat16 [48, 48, 48, 128], P('space'), may hold values from -6 to 6
Outputs:
- handed: bfloat16 [1536, 48, 48, 128], P(('tm', 'space'))
- projection: float32 [1024, 32], P('tm')
The draws below stay inside these ranges and needn't reach their ends.
All inputs are finite; a program needn't handle non-finite values.
Results may differ from the reference program's by a relative error of at most 0.006.
Values may be sent and summed in bfloat16 or wider, within the bound.
A program may use at most 64 MiB of HBM per device.

```python
import math
import jax
import jax.numpy as jnp
from jax import lax

L = 48
C4 = 4
ORB = 32
SECTIONS = 32
ROWS = 1536


def draw_blocks(key, part):
    key = jax.random.fold_in(key, 11)
    row_index = jnp.arange(SECTIONS * L, dtype=jnp.int32) % L
    position = row_index.astype(jnp.float32) / (L - 1)
    extent = (SECTIONS * L, L, L, C4 * ORB)
    values = jax.random.truncated_normal(key, -4.0, 4.0, extent, jnp.float32)
    profile = 1.0 + 2.0 * position
    return (values * profile[:, None, None, None]).astype(jnp.bfloat16)


def levels(stream_key, dims, pieces, low, largest):
    level = 1.0
    for dim, blocks in pieces:
        steps = jax.random.uniform(jax.random.fold_in(jax.random.fold_in(stream_key, 6), dim), (blocks,), jnp.float32, low / len(pieces), largest / len(pieces))
        level = level * jnp.repeat(jnp.exp(steps), dims[dim] // blocks).reshape((-1,) + (1,) * (len(dims) - 1 - dim))
    return level


def bell_draw(key, shape, scale, most, cuts=(), kind=jnp.bfloat16):
    entries = scale * jax.random.normal(key, shape, jnp.float32)
    if cuts:
        entries = entries * levels(key, shape, cuts, -0.22, 0.18)
    return jnp.clip(entries, -most, most).astype(kind)


def setup_inputs(seed: int = 0) -> dict:
    streams_of = jax.random.split(jax.random.key(seed), 4)
    blocks = draw_blocks(jax.random.fold_in(streams_of[3], 71), 0)
    fields = bell_draw(streams_of[1], (ROWS, L, 3 * L), 1.0, 4.0, ((0, 512),), jnp.float32)
    trial = bell_draw(streams_of[2], (L, L, L, C4 * ORB), 1.0, 6.0, ((0, 16),))
    return {"blocks": blocks, "fields": fields, "trial": trial}


KINETIC = 0.0716
MIX_SCALAR = 0.25
MIX_ISOSPIN = 0.15

def mixing(wavefn, auxiliary):
    length = wavefn.shape[2]
    scalar = auxiliary[..., :length][..., None]
    flavour = auxiliary[..., length:2 * length][..., None]
    charge = auxiliary[..., 2 * length:][..., None]
    midpoint = wavefn.shape[3] // 2
    lower_iso = wavefn[..., :midpoint]
    upper_iso = wavefn[..., midpoint:]
    diagonal_term = 1.0 + MIX_SCALAR * scalar
    new_lower = (diagonal_term + MIX_ISOSPIN * charge) * lower_iso + MIX_ISOSPIN * flavour * upper_iso
    new_upper = (diagonal_term - MIX_ISOSPIN * charge) * upper_iso + MIX_ISOSPIN * flavour * lower_iso
    return jnp.concatenate([new_lower, new_upper], axis=3)

def reference(blocks, fields, trial):
    full_momenta = 2.0 * math.pi * jnp.fft.fftfreq(L).astype(jnp.float32)
    half_momenta = 2.0 * math.pi * jnp.fft.rfftfreq(L).astype(jnp.float32)
    squared = full_momenta[:, None, None] ** 2 + full_momenta[None, :, None] ** 2 + half_momenta[None, None, :] ** 2
    damping = jnp.exp(-0.5 * KINETIC * squared).astype(jnp.float32)

    def kinetic(wavefn):
        spectrum = jnp.fft.rfftn(wavefn, axes=(0, 1, 2))
        result = jnp.fft.irfftn(spectrum * damping[..., None], s=(L, L, L), axes=(0, 1, 2))
        return result.astype(jnp.float32)

    def one_section(section_index):
        row_start = (section_index * L).astype(jnp.int32)
        following = ((section_index + 1) % SECTIONS * L).astype(jnp.int32)
        orbital_block = lax.dynamic_slice_in_dim(blocks, row_start, L, 0).astype(jnp.float32)
        own_field = lax.dynamic_slice_in_dim(fields, row_start, L, 0)
        next_field = lax.dynamic_slice_in_dim(fields, following, L, 0)
        current = mixing(kinetic(orbital_block), own_field)
        current = mixing(kinetic(current), next_field)
        sites_all = L * L * L
        products = jnp.einsum('nco,ncp->op', trial.reshape(sites_all, C4, ORB).astype(jnp.float32), current.reshape(sites_all, C4, ORB), precision=lax.Precision.HIGHEST)
        products = products / math.sqrt(C4 * L ** 3)
        return (current.astype(jnp.bfloat16), products)
    advanced, projections = lax.map(one_section, jnp.arange(SECTIONS, dtype=jnp.int32))
    handed = jnp.roll(advanced, 2, axis=0).reshape(SECTIONS * L, L, L, C4 * ORB)
    return (handed, projections.reshape(SECTIONS * ORB, ORB))
```

```python
import math

import jax
import jax.numpy as jnp
import ml_dtypes
import numpy as np
from jax import lax
from jax.experimental import pallas as pl
from jax.experimental.pallas import tpu as pltpu
from jax.sharding import PartitionSpec as P

L = 48
C4 = 4
ORB = 32
K = C4 * ORB

KINETIC = 0.0716
MIX_SCALAR = 0.25
MIX_ISOSPIN = 0.15

TM = 32
GRID = 4
SPACE = GRID * GRID
R = L // SPACE
ZS = 16
G = L // ZS
ROWS = L * ZS
TRI = G * R * ZS
MESH = pl.DeviceIdType.MESH


def tables():
    modes = np.arange(L) - L // 2
    damping = np.exp(-0.5 * KINETIC * (2 * math.pi / L * modes) ** 2)
    sites = np.arange(L)
    offset = sites[:, None] - sites[None, :]
    kernel = (damping[:, None, None] * np.cos(2 * math.pi / L * modes[:, None, None] * offset)).sum(0) / L
    diagonal = float(kernel[0, 0])
    unit = kernel / diagonal

    major = np.kron(unit, np.eye(ZS))
    minor = np.einsum("azbw,xy->axzbyw", unit.reshape(G, ZS, G, ZS), np.eye(R)).reshape(TRI, TRI)

    lanes = np.zeros((3 * L, 3 * K))
    for z in range(L):
        lanes[z, z] = 1
        lanes[2 * L + z, L + z] = 1
        lanes[L + z, K + z] = 1
        lanes[L + z, 2 * K + L + z] = 1
    pack = np.zeros((SPACE, 16, 3, R, L))
    for j in range(SPACE):
        for x in range(R):
            for y in range(R):
                n = x * R + y
                pack[j, n, 0, x, R * j + y] = 1
                pack[j, 9 + n // 2, 1 + n % 2, x, R * j + y] = 1
    pack = pack.reshape(SPACE * 16, 3 * R * L)
    pick = np.zeros((2, R, G, R, ZS, 16))
    keep = np.zeros((2, R, G, R, ZS, K))
    for y in range(R):
        for x in range(R):
            n = x * R + y
            pick[0, y, :, x, :, n] = 1
            pick[1, y, :, x, :, 9 + n // 2] = 1
            for g in range(G):
                for z in range(ZS):
                    keep[0, y, g, x, z, [ZS * g + z, L + ZS * g + z]] = 1
                    keep[1, y, g, x, z, L * (n % 2) + ZS * g + z] = 1
    pick = pick.reshape(2 * R * TRI, 16)
    keep = keep.reshape(2 * R * TRI, K)
    spread = np.kron(np.eye(L), np.ones((ZS, 1)))
    keep_z = np.zeros((G, ZS, 2 * K))
    for g in range(G):
        for z in range(ZS):
            keep_z[g, z, [ZS * g + z, L + ZS * g + z, K + ZS * g + z]] = 1
    fill = np.zeros((2 * K, 2 * K))
    fill[:L, :K] = 1
    fill[L : 2 * L, : K // 2] = 1
    fill[L : 2 * L, K // 2 : K] = -1
    fill[K : K + 2 * L, K:] = 1
    bf16 = lambda a: np.asarray(a, np.float32).astype(ml_dtypes.bfloat16)
    f32 = lambda a: np.asarray(a, np.float32)
    mats = [bf16(major), bf16(minor), bf16(lanes), bf16(pack), bf16(pick), f32(keep), bf16(spread), f32(keep_z), bf16(fill)]
    return diagonal, mats


def dot(a, b):
    return jnp.dot(a, b, preferred_element_type=jnp.float32)


def lanes3(parts):
    return jnp.concatenate(parts, axis=1)


def turn(value, shift):
    return pltpu.roll(value, shift, axis=1)


def kernel(
    diagonal,
    blocks, fields, trial, major, minor, lanes, pack, pick, keep, spread, keep_z, fill,
    handed, projection,
    w_in, s1, y1, t1, t2, s2, x2, out_v, trial_v, fx_s, fx_r, fy_s, fy_r, fy, c1, c2,
    prod, p_s, p_r, q_s, q_r,
    z_send, z_recv, s1_send, y1_recv, s2_send, x2_recv, o_send, o_recv, tr_sem,
    fx_sem, fy_sem, ff_sem, p_sem, q_sem,
):
    bf16 = jnp.bfloat16
    tm = lax.axis_index("tm")
    sp = lax.axis_index("space")
    odd = lax.rem(tm, 2)
    even = odd == 0
    up = lax.rem(tm + 2, TM)
    down = lax.rem(tm + TM - 2, TM)
    beside = lax.rem(tm + TM - 1 + 2 * odd, TM)
    my_y = sp // GRID
    my_x = lax.rem(sp, GRID)
    cube = diagonal**3

    def peer(k):
        return lax.rem(my_y + k // GRID, GRID) * GRID + lax.rem(my_x + lax.rem(k, GRID), GRID)

    def remote(src, dst, send, recv, device):
        return pltpu.make_async_remote_copy(
            src_ref=src, dst_ref=dst, send_sem=send, recv_sem=recv, device_id=device, device_id_type=MESH
        )

    def to_peers(copy):
        @pl.loop(1, SPACE)
        def _(k):
            copy(peer(k))

    def arrived(ref, sem):
        pltpu.make_async_copy(ref, ref, sem).wait()

    barrier = pltpu.get_barrier_semaphore()

    def greet(device):
        pl.semaphore_signal(barrier, inc=1, device_id=device, device_id_type=MESH)

    to_peers(lambda j: greet((tm, j)))
    for other in (up, down, beside):
        greet((other, sp))
    pl.semaphore_wait(barrier, SPACE + 2)

    def hand(g):
        for x in range(R):
            remote(
                blocks.at[x, :, pl.ds(g * ZS, ZS), :], w_in.at[g, x], z_send.at[g], z_recv.at[g], (up, sp)
            ).start()

    @pl.when(even)
    def _():
        hand(0)
        hand(1)

    @pl.when(odd == 1)
    def _():
        for g in range(G):
            for x in range(R):
                pltpu.make_async_copy(blocks.at[x, :, pl.ds(g * ZS, ZS), :], w_in.at[g, x], z_recv.at[g]).start()

    lane = lax.broadcasted_iota(jnp.int32, (1, 3 * L), 1)
    scale = jnp.where(lane < L, cube * MIX_SCALAR, cube * MIX_ISOSPIN)
    scaled = (fields[...].reshape(R * L, 3 * L) * scale).astype(bf16)
    placed = dot(scaled, lanes[...]).astype(bf16)
    fx_s[0] = placed[:, :K].reshape(R, L, K)
    fx_s[1] = placed[:, K : 2 * K].reshape(R, L, K)
    stacked = jnp.concatenate([placed[:, :K], placed[:, K : 2 * K], placed[:, 2 * K :]], axis=0)
    fy_s[...] = dot(pack[...], stacked).astype(bf16).reshape(SPACE, 16, K)
    fy_r[sp] = fy_s[sp]
    remote(fx_s, fx_r, fx_sem.at[0], fx_sem.at[1], (beside, sp)).start()
    to_peers(lambda j: remote(fy_s.at[j], fy_r.at[sp], fy_sem.at[0], fy_sem.at[1], (tm, j)).start())

    for g in range(G):
        for x in range(R):
            pltpu.make_async_copy(trial.at[x, :, pl.ds(g * ZS, ZS), :], trial_v.at[g, x], tr_sem).start()

    @pl.when(even)
    def _():
        arrived(fy_r.at[pl.ds(0, SPACE - 1)], fy_sem.at[1])
        remote(fy_r, fy, ff_sem.at[0], ff_sem.at[1], (up, sp)).start()

    def coefficients():
        @pl.when(even)
        def _():
            arrived(fy, ff_sem.at[1])

        @pl.when(odd == 1)
        def _():
            arrived(fy_r.at[pl.ds(0, SPACE - 1)], fy_sem.at[1])
            fy[...] = fy_r[...]

        top = lax.broadcasted_iota(jnp.int32, (1, 2 * K), 1)
        constant = jnp.where(top < K, cube, 0.0)

        @pl.loop(0, SPACE)
        def _(i):
            rows = (dot(pick[...], fy[i]) * keep[...]).astype(bf16)
            both = lanes3([rows[: R * TRI], rows[R * TRI :]])
            c1[i] = dot(both, fill[...]) + constant

        arrived(fx_r, fx_sem.at[1])

        @pl.loop(0, R)
        def _(x):
            rows = dot(spread[...], lanes3([fx_r[0, x], fx_r[1, x]])).reshape(L, ZS, 2 * K)
            for g in range(G):
                mine = (rows * keep_z[g][None]).reshape(ROWS, 2 * K).astype(bf16)
                c2[g, x] = dot(mine, fill[...]) + constant

    @pl.loop(0, G + 1)
    def _(t):
        @pl.when(t < G)
        def _():
            g = t
            arrived(w_in.at[g], z_recv.at[g])

            @pl.when(jnp.logical_and(even, g == 0))
            def _():
                hand(2)

            moved = dot(major[...], lanes3([w_in[g, x].reshape(ROWS, K) for x in range(R)])).astype(bf16)
            for x in range(R):
                s1[g, x] = moved[:, x * K : (x + 1) * K].reshape(L, ZS, K)
            y1[g, pl.ds(sp * R, R)] = s1[g, :, pl.ds(sp * R, R)]
            to_peers(
                lambda j: remote(
                    s1.at[g, :, pl.ds(j * R, R)], y1.at[g, pl.ds(sp * R, R)], s1_send.at[g], y1_recv.at[g], (tm, j)
                ).start()
            )

        @pl.when(t == 1)
        def _():
            coefficients()

        @pl.when(t > 0)
        def _():
            g = t - 1
            arrived(y1.at[g, pl.ds(0, L - R)], y1_recv.at[g])
            moved = dot(major[...], lanes3([y1[g, :, y].reshape(ROWS, K) for y in range(R)])).astype(bf16)
            for y in range(R):
                t1[g, y] = moved[:, y * K : (y + 1) * K].reshape(L, ZS, K)

    @pl.loop(0, SPACE)
    def _(i):
        def column(y):
            return jnp.concatenate([t1[g, y, pl.ds(i * R, R)].reshape(R * ZS, K) for g in range(G)], axis=0)

        moved = dot(minor[...], lanes3([column(y) for y in range(R)]))
        mixed = []
        for y in range(R):
            own = moved[:, y * K : (y + 1) * K]
            coefs = c1[i, y * TRI : (y + 1) * TRI]
            mixed.append((coefs[:, :K] * own + coefs[:, K:] * turn(own, K // 2)).astype(bf16))
        again = dot(minor[...], lanes3(mixed)).astype(bf16)
        for y in range(R):
            for g in range(G):
                t2[g, y, pl.ds(i * R, R)] = again[
                    g * R * ZS : (g + 1) * R * ZS, y * K : (y + 1) * K
                ].reshape(R, ZS, K)

    @pl.loop(0, G)
    def _(g):
        moved = dot(major[...], lanes3([t2[g, y].reshape(ROWS, K) for y in range(R)])).astype(bf16)
        for y in range(R):
            s2[g, :, y] = moved[:, y * K : (y + 1) * K].reshape(L, ZS, K)
        x2[g, :, pl.ds(sp * R, R)] = s2[g, pl.ds(sp * R, R)]
        to_peers(
            lambda j: remote(
                s2.at[g, pl.ds(j * R, R)], x2.at[g, :, pl.ds(sp * R, R)], s2_send.at[g], x2_recv.at[g], (tm, j)
            ).start()
        )

    prod[...] = jnp.zeros_like(prod)
    arrived(trial_v, tr_sem)

    @pl.loop(0, G)
    def _(g):
        arrived(x2.at[g, :, pl.ds(0, L - R)], x2_recv.at[g])
        moved = dot(major[...], lanes3([x2[g, x].reshape(ROWS, K) for x in range(R)]))
        for x in range(R):
            own = moved[:, x * K : (x + 1) * K]
            coefs = c2[g, x]
            mixed = (coefs[:, :K] * own + coefs[:, K:] * turn(own, K // 2)).astype(bf16)
            out_v[g, x] = mixed.reshape(L, ZS, K)
            target = handed.at[x, :, pl.ds(g * ZS, ZS), :]

            @pl.when(even)
            def _():
                pltpu.make_async_copy(out_v.at[g, x], target, o_recv).start()

            @pl.when(odd == 1)
            def _():
                remote(out_v.at[g, x], target, o_send, o_recv, (up, sp)).start()

            prod[...] += lax.dot_general(
                trial_v[g, x].reshape(ROWS, K), mixed, (((0,), (0,)), ((), ())), preferred_element_type=jnp.float32
            )

    total = prod[:ORB]
    for c in range(1, C4):
        total = total + turn(prod[c * ORB : (c + 1) * ORB], K - c * ORB)
    quarter = lax.broadcasted_iota(jnp.int32, (8, K), 1) // ORB
    packed = jnp.where(quarter == 0, total[:8], 0.0)
    for q in range(1, 4):
        packed = packed + jnp.where(quarter == q, turn(total[8 * q : 8 * q + 8], q * ORB), 0.0)
    p_s[...] = packed
    p_r[sp] = packed
    to_peers(lambda j: remote(p_s, p_r.at[sp], p_sem.at[0], p_sem.at[1], (tm, j)).start())
    arrived(p_r.at[pl.ds(0, SPACE - 1)], p_sem.at[1])
    q_s[...] = jnp.sum(p_r[...], axis=0) * (1.0 / math.sqrt(C4 * L**3))

    @pl.when(even)
    def _():
        remote(q_s, q_r, q_sem.at[0], q_sem.at[1], (down, sp)).start()
        arrived(q_r, q_sem.at[1])

    @pl.when(odd == 1)
    def _():
        q_r[...] = q_s[...]

    result = q_r[...]
    for q in range(4):
        rows = result if q == 0 else turn(result, K - q * ORB)
        projection[8 * q : 8 * q + 8, :] = rows[:, :ORB]

    arrived(fx_s, fx_sem.at[0])
    arrived(fy_s.at[pl.ds(0, SPACE - 1)], fy_sem.at[0])
    arrived(p_r.at[pl.ds(0, SPACE - 1)], p_sem.at[0])
    for g in range(G):
        arrived(s1.at[g, :, pl.ds(0, L - R)], s1_send.at[g])
        arrived(s2.at[g, pl.ds(0, L - R)], s2_send.at[g])

    @pl.when(even)
    def _():
        for g in range(G):
            arrived(w_in.at[g], z_send.at[g])
        arrived(fy_r, ff_sem.at[0])
        arrived(q_s, q_sem.at[0])

    @pl.when(odd == 1)
    def _():
        arrived(out_v, o_send)

    arrived(out_v, o_recv)


def body(blocks, fields, trial):
    diagonal, mats = tables()
    bf16, f32 = jnp.bfloat16, jnp.float32
    vmem = pl.BlockSpec(memory_space=pltpu.VMEM)
    hbm = pl.BlockSpec(memory_space=pl.ANY)
    dma = pltpu.SemaphoreType.DMA
    by_x = pltpu.VMEM((G, R, L, ZS, K), bf16)
    by_pair = pltpu.VMEM((G, L, R, ZS, K), bf16)
    packed = pltpu.VMEM((SPACE, 16, K), bf16)
    tile = pltpu.VMEM((8, K), f32)
    scratch = [
        by_x, by_x, by_pair, by_x, by_x, by_pair, by_x, by_x, by_x,
        pltpu.VMEM((2, R, L, K), bf16), pltpu.VMEM((2, R, L, K), bf16),
        packed, packed, packed,
        pltpu.VMEM((SPACE, R * TRI, 2 * K), f32), pltpu.VMEM((G, R, ROWS, 2 * K), f32),
        pltpu.VMEM((K, K), f32), tile, pltpu.VMEM((SPACE, 8, K), f32), tile, tile,
        dma((G,)), dma((G,)), dma((G,)), dma((G,)), dma((G,)), dma((G,)), dma(()), dma(()), dma(()),
        dma((2,)), dma((2,)), dma((2,)), dma((2,)), dma((2,)),
    ]
    return pl.pallas_call(
        lambda *refs: kernel(diagonal, *refs),
        out_shape=(
            jax.ShapeDtypeStruct(blocks.shape, bf16),
            jax.ShapeDtypeStruct((ORB, ORB), f32),
        ),
        in_specs=[hbm, vmem, hbm] + [vmem] * len(mats),
        out_specs=(hbm, vmem),
        scratch_shapes=scratch,
        compiler_params=pltpu.CompilerParams(
            collective_id=0, has_side_effects=True, vmem_limit_bytes=56 * 1024 * 1024
        ),
    )(blocks, fields, trial, *[jnp.asarray(m) for m in mats])


def solution(mesh):
    in_specs = (
        P(("tm", "space"), None, None, None),
        P(("tm", "space"), None, None),
        P("space", None, None, None),
    )
    out_specs = (P(("tm", "space"), None, None, None), P("tm", None))
    return jax.shard_map(body, mesh=mesh, in_specs=in_specs, out_specs=out_specs, check_vma=False)
```

```python
import math

import jax
import jax.numpy as jnp
import ml_dtypes
import numpy as np
from jax import lax
from jax.experimental import pallas as pl
from jax.experimental.pallas import tpu as pltpu
from jax.sharding import PartitionSpec as P

L = 48
C4 = 4
ORB = 32
K = C4 * ORB

KINETIC = 0.0716
MIX_SCALAR = 0.25
MIX_ISOSPIN = 0.15

TM = 32
GRID = 4
SPACE = GRID * GRID
R = L // SPACE
ZS = 16
G = L // ZS
ROWS = L * ZS
TRI = G * R * ZS
MESH = pl.DeviceIdType.MESH


def tables():
    modes = np.arange(L) - L // 2
    damping = np.exp(-0.5 * KINETIC * (2 * math.pi / L * modes) ** 2)
    sites = np.arange(L)
    offset = sites[:, None] - sites[None, :]
    kernel = (damping[:, None, None] * np.cos(2 * math.pi / L * modes[:, None, None] * offset)).sum(0) / L
    diagonal = float(kernel[0, 0])
    unit = kernel / diagonal

    major = np.kron(unit, np.eye(ZS))
    minor = np.einsum("azbw,xy->axzbyw", unit.reshape(G, ZS, G, ZS), np.eye(R)).reshape(TRI, TRI)

    lanes = np.zeros((3 * L, 3 * K))
    for z in range(L):
        lanes[z, z] = 1
        lanes[2 * L + z, L + z] = 1
        lanes[L + z, K + z] = 1
        lanes[L + z, 2 * K + L + z] = 1
    pack = np.zeros((SPACE, 16, 3, R, L))
    for j in range(SPACE):
        for x in range(R):
            for y in range(R):
                n = x * R + y
                pack[j, n, 0, x, R * j + y] = 1
                pack[j, 9 + n // 2, 1 + n % 2, x, R * j + y] = 1
    pack = pack.reshape(SPACE * 16, 3 * R * L)
    pick = np.zeros((2, R, G, R, ZS, 16))
    keep = np.zeros((2, R, G, R, ZS, K))
    for y in range(R):
        for x in range(R):
            n = x * R + y
            pick[0, y, :, x, :, n] = 1
            pick[1, y, :, x, :, 9 + n // 2] = 1
            for g in range(G):
                for z in range(ZS):
                    keep[0, y, g, x, z, [ZS * g + z, L + ZS * g + z]] = 1
                    keep[1, y, g, x, z, L * (n % 2) + ZS * g + z] = 1
    pick = pick.reshape(2 * R * TRI, 16)
    keep = keep.reshape(2 * R * TRI, K)
    spread = np.kron(np.eye(L), np.ones((ZS, 1)))
    keep_z = np.zeros((G, ZS, 2 * K))
    for g in range(G):
        for z in range(ZS):
            keep_z[g, z, [ZS * g + z, L + ZS * g + z, K + ZS * g + z]] = 1
    fill = np.zeros((2 * K, 2 * K))
    fill[:L, :K] = 1
    fill[L : 2 * L, : K // 2] = 1
    fill[L : 2 * L, K // 2 : K] = -1
    fill[K : K + 2 * L, K:] = 1
    bf16 = lambda a: np.asarray(a, np.float32).astype(ml_dtypes.bfloat16)
    f32 = lambda a: np.asarray(a, np.float32)
    mats = [bf16(major), bf16(minor), bf16(lanes), bf16(pack), bf16(pick), f32(keep), bf16(spread), f32(keep_z), bf16(fill)]
    return diagonal, mats


def dot(a, b):
    return jnp.dot(a, b, preferred_element_type=jnp.float32)


def lanes3(parts):
    return jnp.concatenate(parts, axis=1)


def turn(value, shift):
    return pltpu.roll(value, shift, axis=1)


def kernel(
    diagonal,
    blocks, fields, trial, major_h, minor_h, lanes_h, pack_h, pick_h, keep_h, spread_h, keep_z_h, fill_h,
    handed, projection,
    fields_v, major, minor, lanes, pack, pick, keep, spread, keep_z, fill,
    w_in, s1, y1, t1, t2, s2, x2, out_v, trial_v, fx_s, fx_r, fy_s, fy_r, fy, c1, c2,
    prod, p_s, p_r, q_s, q_r,
    z_send, z_recv, s1_send, y1_recv, s2_send, x2_recv, o_send, o_recv, tr_sem,
    fx_sem, fy_sem, ff_sem, p_sem, q_sem, in_sem,
):
    bf16 = jnp.bfloat16
    tm = lax.axis_index("tm")
    sp = lax.axis_index("space")
    odd = lax.rem(tm, 2)
    even = odd == 0
    up = lax.rem(tm + 2, TM)
    down = lax.rem(tm + TM - 2, TM)
    beside = lax.rem(tm + TM - 1 + 2 * odd, TM)
    my_y = sp // GRID
    my_x = lax.rem(sp, GRID)
    cube = diagonal**3

    def peer(k):
        return lax.rem(my_y + k // GRID, GRID) * GRID + lax.rem(my_x + lax.rem(k, GRID), GRID)

    def remote(src, dst, send, recv, device):
        return pltpu.make_async_remote_copy(
            src_ref=src, dst_ref=dst, send_sem=send, recv_sem=recv, device_id=device, device_id_type=MESH
        )

    def to_peers(copy):
        @pl.loop(1, SPACE)
        def _(k):
            copy(peer(k))

    def arrived(ref, sem):
        pltpu.make_async_copy(ref, ref, sem).wait()

    inputs = [
        pltpu.make_async_copy(src, dst, in_sem.at[n])
        for n, (src, dst) in enumerate(
            zip(
                (fields, lanes_h, pack_h, major_h, minor_h, pick_h, keep_h, spread_h, keep_z_h, fill_h),
                (fields_v, lanes, pack, major, minor, pick, keep, spread, keep_z, fill),
            )
        )
    ]
    for copy in inputs:
        copy.start()

    barrier = pltpu.get_barrier_semaphore()

    def greet(device):
        pl.semaphore_signal(barrier, inc=1, device_id=device, device_id_type=MESH)

    for other in (up, down, beside):
        greet((other, sp))
    to_peers(lambda j: greet((tm, j)))

    @pl.when(odd == 1)
    def _():
        for g in range(G):
            for x in range(R):
                pltpu.make_async_copy(blocks.at[x, :, pl.ds(g * ZS, ZS), :], w_in.at[g, x], z_recv.at[g]).start()

    for copy in inputs:
        copy.wait()
    lane = lax.broadcasted_iota(jnp.int32, (1, 3 * L), 1)
    scale = jnp.where(lane < L, cube * MIX_SCALAR, cube * MIX_ISOSPIN)
    scaled = (fields_v[...].reshape(R * L, 3 * L) * scale).astype(bf16)
    placed = dot(scaled, lanes[...]).astype(bf16)
    fx_s[0] = placed[:, :K].reshape(R, L, K)
    fx_s[1] = placed[:, K : 2 * K].reshape(R, L, K)
    stacked = jnp.concatenate([placed[:, :K], placed[:, K : 2 * K], placed[:, 2 * K :]], axis=0)
    fy_s[...] = dot(pack[...], stacked).astype(bf16).reshape(SPACE, 16, K)
    fy_r[sp] = fy_s[sp]

    pl.semaphore_wait(barrier, SPACE + 2)

    def hand(g):
        for x in range(R):
            remote(
                blocks.at[x, :, pl.ds(g * ZS, ZS), :], w_in.at[g, x], z_send.at[g], z_recv.at[g], (up, sp)
            ).start()

    @pl.when(even)
    def _():
        hand(0)
        hand(1)

    to_peers(lambda j: remote(fy_s.at[j], fy_r.at[sp], fy_sem.at[0], fy_sem.at[1], (tm, j)).start())
    remote(fx_s, fx_r, fx_sem.at[0], fx_sem.at[1], (beside, sp)).start()

    for g in range(G):
        for x in range(R):
            pltpu.make_async_copy(trial.at[x, :, pl.ds(g * ZS, ZS), :], trial_v.at[g, x], tr_sem).start()

    @pl.when(even)
    def _():
        arrived(fy_r.at[pl.ds(0, SPACE - 1)], fy_sem.at[1])
        remote(fy_r, fy, ff_sem.at[0], ff_sem.at[1], (up, sp)).start()

    def coefficients():
        @pl.when(even)
        def _():
            arrived(fy, ff_sem.at[1])

        @pl.when(odd == 1)
        def _():
            arrived(fy_r.at[pl.ds(0, SPACE - 1)], fy_sem.at[1])
            fy[...] = fy_r[...]

        top = lax.broadcasted_iota(jnp.int32, (1, 2 * K), 1)
        constant = jnp.where(top < K, cube, 0.0)

        @pl.loop(0, SPACE)
        def _(i):
            rows = (dot(pick[...], fy[i]) * keep[...]).astype(bf16)
            both = lanes3([rows[: R * TRI], rows[R * TRI :]])
            c1[i] = (dot(both, fill[...]) + constant).reshape(R, TRI, 2 * K)

        arrived(fx_r, fx_sem.at[1])

        @pl.loop(0, R)
        def _(x):
            rows = dot(spread[...], lanes3([fx_r[0, x], fx_r[1, x]])).reshape(L, ZS, 2 * K)
            for g in range(G):
                mine = (rows * keep_z[g][None]).reshape(ROWS, 2 * K).astype(bf16)
                c2[g, x] = dot(mine, fill[...]) + constant

    @pl.loop(0, G)
    def _(g):
        arrived(w_in.at[g], z_recv.at[g])

        @pl.when(jnp.logical_and(even, g == 0))
        def _():
            hand(2)

        moved = dot(major[...], lanes3([w_in[g, x].reshape(ROWS, K) for x in range(R)])).astype(bf16)
        for x in range(R):
            s1[g, x] = moved[:, x * K : (x + 1) * K].reshape(L, ZS, K)

        @pl.when(g < G - 1)
        def _():
            to_peers(
                lambda j: remote(
                    s1.at[g, :, pl.ds(j * R, R)], y1.at[g, pl.ds(sp * R, R)], s1_send.at[g], y1_recv.at[g], (tm, j)
                ).start()
            )

        @pl.when(g == G - 1)
        def _():
            for y in range(R):
                to_peers(
                    lambda j: remote(
                        s1.at[g, :, j * R + y], y1.at[g, pl.ds(sp * R, R), y], s1_send.at[g], y1_recv.at[g + y], (tm, j)
                    ).start()
                )

        y1[g, pl.ds(sp * R, R)] = s1[g, :, pl.ds(sp * R, R)]

        @pl.when(g == 2 * odd)
        def _():
            coefficients()

    @pl.loop(0, R)
    def _(y):
        @pl.when(y == 0)
        def _():
            for g in range(G - 1):
                arrived(y1.at[g, pl.ds(0, L - R)], y1_recv.at[g])

        arrived(y1.at[G - 1, pl.ds(0, L - R), y], y1_recv.at[G - 1 + y])
        moved = dot(major[...], lanes3([y1[g, :, y].reshape(ROWS, K) for g in range(G)])).astype(bf16)
        for g in range(G):
            t1[g] = moved[:, g * K : (g + 1) * K].reshape(L, ZS, K)

        def pair(n, carry):
            def column(i):
                return jnp.concatenate([t1[g, pl.ds(i * R, R)].reshape(R * ZS, K) for g in range(G)], axis=0)

            both = dot(minor[...], lanes3([column(2 * n), column(2 * n + 1)]))
            mixed = []
            for m in range(2):
                own = both[:, m * K : (m + 1) * K]
                coefs = c1[2 * n + m, y]
                mixed.append((coefs[:, :K] * own + coefs[:, K:] * turn(own, K // 2)).astype(bf16))
            again = dot(minor[...], lanes3(mixed)).astype(bf16)
            for m in range(2):
                for g in range(G):
                    t2[g, pl.ds((2 * n + m) * R, R)] = again[
                        g * R * ZS : (g + 1) * R * ZS, m * K : (m + 1) * K
                    ].reshape(R, ZS, K)
            return carry

        lax.fori_loop(0, SPACE // 2, pair, 0, unroll=4)

        moved = dot(major[...], lanes3([t2[g].reshape(ROWS, K) for g in range(G)])).astype(bf16)
        for g in range(G):
            s2[y, g] = moved[:, g * K : (g + 1) * K].reshape(L, ZS, K)

        @pl.when(y < R - 1)
        def _():
            to_peers(
                lambda j: remote(
                    s2.at[y, :, pl.ds(j * R, R)], x2.at[:, :, sp * R + y], s2_send.at[y], x2_recv.at[y], (tm, j)
                ).start()
            )

        @pl.when(y == R - 1)
        def _():
            for g in range(G):
                to_peers(
                    lambda j: remote(
                        s2.at[y, g, pl.ds(j * R, R)], x2.at[g, :, sp * R + y], s2_send.at[y], x2_recv.at[y + g], (tm, j)
                    ).start()
                )

        x2[:, :, sp * R + y] = s2[y, :, pl.ds(sp * R, R)]

    prod[...] = jnp.zeros_like(prod)
    arrived(trial_v, tr_sem)
    for y in range(R - 1):
        arrived(x2.at[:, :, pl.ds(0, SPACE - 1)], x2_recv.at[y])

    @pl.loop(0, G)
    def _(g):
        arrived(x2.at[g, :, pl.ds(0, SPACE - 1)], x2_recv.at[R - 1 + g])
        moved = dot(major[...], lanes3([x2[g, x].reshape(ROWS, K) for x in range(R)]))
        for x in range(R):
            own = moved[:, x * K : (x + 1) * K]
            coefs = c2[g, x]
            mixed = (coefs[:, :K] * own + coefs[:, K:] * turn(own, K // 2)).astype(bf16)
            out_v[g, x] = mixed.reshape(L, ZS, K)
            target = handed.at[x, :, pl.ds(g * ZS, ZS), :]

            @pl.when(even)
            def _():
                pltpu.make_async_copy(out_v.at[g, x], target, o_recv).start()

            @pl.when(odd == 1)
            def _():
                remote(out_v.at[g, x], target, o_send, o_recv, (up, sp)).start()

        for x in range(R):
            prod[...] += lax.dot_general(
                trial_v[g, x].reshape(ROWS, K),
                out_v[g, x].reshape(ROWS, K),
                (((0,), (0,)), ((), ())),
                preferred_element_type=jnp.float32,
            )

    total = prod[:ORB]
    for c in range(1, C4):
        total = total + turn(prod[c * ORB : (c + 1) * ORB], K - c * ORB)
    quarter = lax.broadcasted_iota(jnp.int32, (8, K), 1) // ORB
    packed = jnp.where(quarter == 0, total[:8], 0.0)
    for q in range(1, 4):
        packed = packed + jnp.where(quarter == q, turn(total[8 * q : 8 * q + 8], q * ORB), 0.0)
    p_s[...] = packed
    p_r[sp] = packed
    to_peers(lambda j: remote(p_s, p_r.at[sp], p_sem.at[0], p_sem.at[1], (tm, j)).start())
    arrived(p_r.at[pl.ds(0, SPACE - 1)], p_sem.at[1])
    q_s[...] = jnp.sum(p_r[...], axis=0) * (1.0 / math.sqrt(C4 * L**3))

    @pl.when(even)
    def _():
        remote(q_s, q_r, q_sem.at[0], q_sem.at[1], (down, sp)).start()
        arrived(q_r, q_sem.at[1])

    @pl.when(odd == 1)
    def _():
        q_r[...] = q_s[...]

    result = q_r[...]
    for q in range(4):
        rows = result if q == 0 else turn(result, K - q * ORB)
        projection[8 * q : 8 * q + 8, :] = rows[:, :ORB]

    arrived(fx_s, fx_sem.at[0])
    arrived(fy_s.at[pl.ds(0, SPACE - 1)], fy_sem.at[0])
    arrived(p_r.at[pl.ds(0, SPACE - 1)], p_sem.at[0])
    for g in range(G):
        arrived(s1.at[g, :, pl.ds(0, L - R)], s1_send.at[g])
        arrived(s2.at[g, :, pl.ds(0, L - R)], s2_send.at[g])

    @pl.when(even)
    def _():
        for g in range(G):
            arrived(w_in.at[g], z_send.at[g])
        arrived(fy_r, ff_sem.at[0])
        arrived(q_s, q_sem.at[0])

    @pl.when(odd == 1)
    def _():
        arrived(out_v, o_send)

    arrived(out_v, o_recv)


def body(blocks, fields, trial):
    diagonal, mats = tables()
    bf16, f32 = jnp.bfloat16, jnp.float32
    vmem = pl.BlockSpec(memory_space=pltpu.VMEM)
    hbm = pl.BlockSpec(memory_space=pl.ANY)
    dma = pltpu.SemaphoreType.DMA
    by_x = pltpu.VMEM((G, R, L, ZS, K), bf16)
    by_pair = pltpu.VMEM((G, L, R, ZS, K), bf16)
    one_row = pltpu.VMEM((G, L, ZS, K), bf16)
    packed = pltpu.VMEM((SPACE, 16, K), bf16)
    tile = pltpu.VMEM((8, K), f32)
    scratch = [pltpu.VMEM(fields.shape, f32)] + [pltpu.VMEM(m.shape, m.dtype) for m in mats]
    scratch += [
        by_x, by_x, by_pair, one_row, one_row, by_x, by_x, by_x, by_x,
        pltpu.VMEM((2, R, L, K), bf16), pltpu.VMEM((2, R, L, K), bf16),
        packed, packed, packed,
        pltpu.VMEM((SPACE, R, TRI, 2 * K), f32), pltpu.VMEM((G, R, ROWS, 2 * K), f32),
        pltpu.VMEM((K, K), f32), tile, pltpu.VMEM((SPACE, 8, K), f32), tile, tile,
        dma((G,)), dma((G,)), dma((G,)), dma((5,)), dma((G,)), dma((5,)), dma(()), dma(()), dma(()),
        dma((2,)), dma((2,)), dma((2,)), dma((2,)), dma((2,)), dma((10,)),
    ]
    return pl.pallas_call(
        lambda *refs: kernel(diagonal, *refs),
        out_shape=(
            jax.ShapeDtypeStruct(blocks.shape, bf16),
            jax.ShapeDtypeStruct((ORB, ORB), f32),
        ),
        in_specs=[hbm] * (3 + len(mats)),
        out_specs=(hbm, vmem),
        scratch_shapes=scratch,
        compiler_params=pltpu.CompilerParams(
            collective_id=0, has_side_effects=True, vmem_limit_bytes=56 * 1024 * 1024
        ),
    )(blocks, fields, trial, *[jnp.asarray(m) for m in mats])


def solution(mesh):
    in_specs = (
        P(("tm", "space"), None, None, None),
        P(("tm", "space"), None, None),
        P("space", None, None, None),
    )
    out_specs = (P(("tm", "space"), None, None, None), P("tm", None))
    return jax.shard_map(body, mesh=mesh, in_specs=in_specs, out_specs=out_specs, check_vma=False)
```

```python
import math

import jax
import jax.numpy as jnp
import ml_dtypes
import numpy as np
from jax import lax
from jax.experimental import pallas as pl
from jax.experimental.pallas import tpu as pltpu
from jax.sharding import PartitionSpec as P

L = 48
C4 = 4
ORB = 32
K = C4 * ORB

KINETIC = 0.0716
MIX_SCALAR = 0.25
MIX_ISOSPIN = 0.15

TM = 32
GRID = 4
SPACE = GRID * GRID
R = L // SPACE
ZS = 16
G = L // ZS
ROWS = L * ZS
TRI = G * R * ZS
MESH = pl.DeviceIdType.MESH


def tables():
    modes = np.arange(L) - L // 2
    damping = np.exp(-0.5 * KINETIC * (2 * math.pi / L * modes) ** 2)
    sites = np.arange(L)
    offset = sites[:, None] - sites[None, :]
    kernel = (damping[:, None, None] * np.cos(2 * math.pi / L * modes[:, None, None] * offset)).sum(0) / L
    diagonal = float(kernel[0, 0])
    unit = kernel / diagonal

    major = np.kron(unit, np.eye(ZS))
    minor = np.einsum("azbw,xy->axzbyw", unit.reshape(G, ZS, G, ZS), np.eye(R)).reshape(TRI, TRI)

    lanes = np.zeros((3 * L, 3 * K))
    for z in range(L):
        lanes[z, z] = 1
        lanes[2 * L + z, L + z] = 1
        lanes[L + z, K + z] = 1
        lanes[L + z, 2 * K + L + z] = 1
    pack = np.zeros((SPACE, 16, 3, R, L))
    for j in range(SPACE):
        for x in range(R):
            for y in range(R):
                n = x * R + y
                pack[j, n, 0, x, R * j + y] = 1
                pack[j, 9 + n // 2, 1 + n % 2, x, R * j + y] = 1
    pack = pack.reshape(SPACE * 16, 3 * R * L)
    pick = np.zeros((2, R, G, R, ZS, 16))
    keep = np.zeros((2, R, G, R, ZS, K))
    for y in range(R):
        for x in range(R):
            n = x * R + y
            pick[0, y, :, x, :, n] = 1
            pick[1, y, :, x, :, 9 + n // 2] = 1
            for g in range(G):
                for z in range(ZS):
                    keep[0, y, g, x, z, [ZS * g + z, L + ZS * g + z]] = 1
                    keep[1, y, g, x, z, L * (n % 2) + ZS * g + z] = 1
    pick = pick.reshape(2 * R * TRI, 16)
    keep = keep.reshape(2 * R * TRI, K)
    spread = np.kron(np.eye(L), np.ones((ZS, 1)))
    keep_z = np.zeros((G, ZS, 2 * K))
    for g in range(G):
        for z in range(ZS):
            keep_z[g, z, [ZS * g + z, L + ZS * g + z, K + ZS * g + z]] = 1
    fill = np.zeros((2 * K, 2 * K))
    fill[:L, :K] = 1
    fill[L : 2 * L, : K // 2] = 1
    fill[L : 2 * L, K // 2 : K] = -1
    fill[K : K + 2 * L, K:] = 1
    bf16 = lambda a: np.asarray(a, np.float32).astype(ml_dtypes.bfloat16)
    f32 = lambda a: np.asarray(a, np.float32)
    mats = [bf16(major), bf16(minor), bf16(lanes), bf16(pack), bf16(pick), f32(keep), bf16(spread), f32(keep_z), bf16(fill)]
    return diagonal, mats


def dot(a, b):
    return jnp.dot(a, b, preferred_element_type=jnp.float32)


def lanes3(parts):
    return jnp.concatenate(parts, axis=1)


def turn(value, shift):
    return pltpu.roll(value, shift, axis=1)


def kernel(
    diagonal,
    blocks, fields, trial, major_h, minor_h, lanes_h, pack_h, pick_h, keep_h, spread_h, keep_z_h, fill_h,
    handed, projection,
    fields_v, major, minor, lanes, pack, pick, keep, spread, keep_z, fill,
    w_in, s1, yh, y1, t1, t2, s2, x2, out_v, trial_v, trial_t, fx_s, fx_r, fy_s, fy_r, fy, c1, c2,
    prod, p_s, p_r, q_s, q_r,
    z_send, z_recv, h_recv, f_send, f_recv, s1_send, y1_recv, s2_send, x2_recv, o_send, o_recv, tr_sem,
    fx_sem, fy_sem, ff_sem, p_sem, q_sem, in_sem,
):
    bf16 = jnp.bfloat16
    tm = lax.axis_index("tm")
    sp = lax.axis_index("space")
    odd = lax.rem(tm, 2)
    even = odd == 0
    up = lax.rem(tm + 2, TM)
    down = lax.rem(tm + TM - 2, TM)
    beside = lax.rem(tm + TM - 1 + 2 * odd, TM)
    my_y = sp // GRID
    my_x = lax.rem(sp, GRID)
    cube = diagonal**3

    def peer(k):
        return lax.rem(my_y + k // GRID, GRID) * GRID + lax.rem(my_x + lax.rem(k, GRID), GRID)

    def remote(src, dst, send, recv, device):
        return pltpu.make_async_remote_copy(
            src_ref=src, dst_ref=dst, send_sem=send, recv_sem=recv, device_id=device, device_id_type=MESH
        )

    def to_peers(copy):
        @pl.loop(1, SPACE)
        def _(k):
            copy(peer(k))

    def arrived(ref, sem):
        pltpu.make_async_copy(ref, ref, sem).wait()

    inputs = [
        pltpu.make_async_copy(src, dst, in_sem.at[n])
        for n, (src, dst) in enumerate(
            zip(
                (fields, lanes_h, pack_h, major_h, minor_h, pick_h, keep_h, spread_h, keep_z_h, fill_h),
                (fields_v, lanes, pack, major, minor, pick, keep, spread, keep_z, fill),
            )
        )
    ]
    for copy in inputs:
        copy.start()

    barrier = pltpu.get_barrier_semaphore()

    def greet(device):
        pl.semaphore_signal(barrier, inc=1, device_id=device, device_id_type=MESH)

    for other in (up, down, beside):
        greet((other, sp))
    to_peers(lambda j: greet((tm, j)))

    def own(g):
        for x in range(R):
            pltpu.make_async_copy(blocks.at[x, :, pl.ds(g * ZS, ZS), :], w_in.at[g, x], z_recv.at[g]).start()

    @pl.when(odd == 1)
    def _():
        for g in range(G - 1):
            own(g)

    own(G - 1)

    for copy in inputs:
        copy.wait()
    lane = lax.broadcasted_iota(jnp.int32, (1, 3 * L), 1)
    scale = jnp.where(lane < L, cube * MIX_SCALAR, cube * MIX_ISOSPIN)
    scaled = (fields_v[...].reshape(R * L, 3 * L) * scale).astype(bf16)
    placed = dot(scaled, lanes[...]).astype(bf16)
    fx_s[0] = placed[:, :K].reshape(R, L, K)
    fx_s[1] = placed[:, K : 2 * K].reshape(R, L, K)
    stacked = jnp.concatenate([placed[:, :K], placed[:, K : 2 * K], placed[:, 2 * K :]], axis=0)
    fy_s[...] = dot(pack[...], stacked).astype(bf16).reshape(SPACE, 16, K)
    fy_r[sp] = fy_s[sp]

    pl.semaphore_wait(barrier, SPACE + 2)

    def hand(g):
        for x in range(R):
            remote(
                blocks.at[x, :, pl.ds(g * ZS, ZS), :], w_in.at[g, x], z_send.at[g], z_recv.at[g], (up, sp)
            ).start()

    @pl.when(even)
    def _():
        hand(0)
        hand(1)

    to_peers(lambda j: remote(fy_s.at[j], fy_r.at[sp], fy_sem.at[0], fy_sem.at[1], (tm, j)).start())
    remote(fx_s, fx_r, fx_sem.at[0], fx_sem.at[1], (beside, sp)).start()

    for g in range(G):
        for x in range(R):
            pltpu.make_async_copy(trial.at[x, :, pl.ds(g * ZS, ZS), :], trial_v.at[g, x], tr_sem).start()

    @pl.when(even)
    def _():
        arrived(fy_r.at[pl.ds(0, SPACE - 1)], fy_sem.at[1])
        remote(fy_r, fy, ff_sem.at[0], ff_sem.at[1], (up, sp)).start()

    def coefficients():
        @pl.when(even)
        def _():
            arrived(fy, ff_sem.at[1])

        @pl.when(odd == 1)
        def _():
            arrived(fy_r.at[pl.ds(0, SPACE - 1)], fy_sem.at[1])
            fy[...] = fy_r[...]

        top = lax.broadcasted_iota(jnp.int32, (1, 2 * K), 1)
        constant = jnp.where(top < K, cube, 0.0)

        @pl.loop(0, SPACE)
        def _(i):
            rows = (dot(pick[...], fy[i]) * keep[...]).astype(bf16)
            both = lanes3([rows[: R * TRI], rows[R * TRI :]])
            c1[i] = (dot(both, fill[...]) + constant).reshape(R, TRI, 2 * K)

        arrived(trial_v, tr_sem)

        @pl.loop(0, G)
        def _(g):
            for x in range(R):
                trial_t[g, :, x * ROWS : (x + 1) * ROWS] = jnp.transpose(trial_v[g, x].reshape(ROWS, K))

        arrived(fx_r, fx_sem.at[1])

        @pl.loop(0, R)
        def _(x):
            rows = dot(spread[...], lanes3([fx_r[0, x], fx_r[1, x]])).reshape(L, ZS, 2 * K)
            for g in range(G):
                mine = (rows * keep_z[g][None]).reshape(ROWS, 2 * K).astype(bf16)
                c2[g, x] = dot(mine, fill[...]) + constant

    def onward(y):
        remote(yh.at[:, y], y1.at[G - 1, :, y], f_send, f_recv.at[y], (up, sp)).start()

    @pl.loop(0, G)
    def _(t):
        g = lax.rem(t + (G - 1) * (1 - odd), G)
        arrived(w_in.at[g], z_recv.at[g])

        @pl.when(jnp.logical_and(even, t == G - 1))
        def _():
            onward(1)
            onward(2)

        moved = dot(major[...], lanes3([w_in[g, x].reshape(ROWS, K) for x in range(R)])).astype(bf16)
        for x in range(R):
            s1[g, x] = moved[:, x * K : (x + 1) * K].reshape(L, ZS, K)

        home = jnp.logical_and(even, t == 0)

        @pl.when(home)
        def _():
            to_peers(
                lambda j: remote(
                    s1.at[g, :, pl.ds(j * R, R)], yh.at[pl.ds(sp * R, R)], s1_send.at[g], h_recv, (tm, j)
                ).start()
            )
            yh[pl.ds(sp * R, R)] = s1[g, :, pl.ds(sp * R, R)]

        @pl.when(jnp.logical_not(home))
        def _():
            @pl.when(t < G - 1)
            def _():
                to_peers(
                    lambda j: remote(
                        s1.at[g, :, pl.ds(j * R, R)], y1.at[g, pl.ds(sp * R, R)], s1_send.at[g], y1_recv.at[g], (tm, j)
                    ).start()
                )

            @pl.when(t == G - 1)
            def _():
                for y in range(R):
                    to_peers(
                        lambda j: remote(
                            s1.at[g, :, j * R + y],
                            y1.at[g, pl.ds(sp * R, R), y],
                            s1_send.at[g],
                            y1_recv.at[G - 1 + y],
                            (tm, j),
                        ).start()
                    )

            y1[g, pl.ds(sp * R, R)] = s1[g, :, pl.ds(sp * R, R)]

        @pl.when(t == (G - 1) * odd)
        def _():
            coefficients()

        @pl.when(jnp.logical_and(even, t == 1))
        def _():
            arrived(yh.at[pl.ds(0, L - R)], h_recv)
            onward(0)

    @pl.loop(0, R)
    def _(y):
        @pl.when(y == 0)
        def _():
            arrived(y1.at[0, pl.ds(0, L - R)], y1_recv.at[0])

        @pl.when(jnp.logical_and(odd == 1, y == 0))
        def _():
            arrived(y1.at[1, pl.ds(0, L - R)], y1_recv.at[1])

        @pl.when(even)
        def _():
            arrived(y1.at[G - 1, :, y], f_recv.at[y])

        arrived(y1.at[G - 1, pl.ds(0, L - R), y], y1_recv.at[G - 1 + y])
        moved = dot(major[...], lanes3([y1[g, :, y].reshape(ROWS, K) for g in range(G)])).astype(bf16)
        for g in range(G):
            t1[g] = moved[:, g * K : (g + 1) * K].reshape(L, ZS, K)

        def pair(n, carry):
            def column(i):
                return jnp.concatenate([t1[g, pl.ds(i * R, R)].reshape(R * ZS, K) for g in range(G)], axis=0)

            both = dot(minor[...], lanes3([column(2 * n), column(2 * n + 1)]))
            mixed = []
            for m in range(2):
                own = both[:, m * K : (m + 1) * K]
                coefs = c1[2 * n + m, y]
                mixed.append((coefs[:, :K] * own + coefs[:, K:] * turn(own, K // 2)).astype(bf16))
            again = dot(minor[...], lanes3(mixed)).astype(bf16)
            for m in range(2):
                for g in range(G):
                    t2[g, pl.ds((2 * n + m) * R, R)] = again[
                        g * R * ZS : (g + 1) * R * ZS, m * K : (m + 1) * K
                    ].reshape(R, ZS, K)
            return carry

        lax.fori_loop(0, SPACE // 2, pair, 0, unroll=4)

        moved = dot(major[...], lanes3([t2[g].reshape(ROWS, K) for g in range(G)])).astype(bf16)
        for g in range(G):
            s2[y, g] = moved[:, g * K : (g + 1) * K].reshape(L, ZS, K)

        @pl.when(y < R - 1)
        def _():
            to_peers(
                lambda j: remote(
                    s2.at[y, :, pl.ds(j * R, R)], x2.at[:, :, sp * R + y], s2_send.at[y], x2_recv.at[y], (tm, j)
                ).start()
            )

        @pl.when(y == R - 1)
        def _():
            for g in range(G):
                to_peers(
                    lambda j: remote(
                        s2.at[y, g, pl.ds(j * R, R)], x2.at[g, :, sp * R + y], s2_send.at[y], x2_recv.at[y + g], (tm, j)
                    ).start()
                )

        x2[:, :, sp * R + y] = s2[y, :, pl.ds(sp * R, R)]

    prod[...] = jnp.zeros_like(prod)
    for y in range(R - 1):
        arrived(x2.at[:, :, pl.ds(0, SPACE - 1)], x2_recv.at[y])

    @pl.loop(0, G)
    def _(g):
        arrived(x2.at[g, :, pl.ds(0, SPACE - 1)], x2_recv.at[R - 1 + g])
        moved = dot(major[...], lanes3([x2[g, x].reshape(ROWS, K) for x in range(R)]))
        for x in range(R):
            own = moved[:, x * K : (x + 1) * K]
            coefs = c2[g, x]
            mixed = (coefs[:, :K] * own + coefs[:, K:] * turn(own, K // 2)).astype(bf16)
            out_v[g, x] = mixed.reshape(L, ZS, K)
            target = handed.at[x, :, pl.ds(g * ZS, ZS), :]

            @pl.when(even)
            def _():
                pltpu.make_async_copy(out_v.at[g, x], target, o_recv).start()

            @pl.when(odd == 1)
            def _():
                remote(out_v.at[g, x], target, o_send, o_recv, (up, sp)).start()

        prod[...] += dot(trial_t[g], out_v[g].reshape(R * ROWS, K))

    total = prod[:ORB]
    for c in range(1, C4):
        total = total + turn(prod[c * ORB : (c + 1) * ORB], K - c * ORB)
    quarter = lax.broadcasted_iota(jnp.int32, (8, K), 1) // ORB
    packed = jnp.where(quarter == 0, total[:8], 0.0)
    for q in range(1, 4):
        packed = packed + jnp.where(quarter == q, turn(total[8 * q : 8 * q + 8], q * ORB), 0.0)
    p_s[...] = packed
    p_r[sp] = packed
    to_peers(lambda j: remote(p_s, p_r.at[sp], p_sem.at[0], p_sem.at[1], (tm, j)).start())
    arrived(p_r.at[pl.ds(0, SPACE - 1)], p_sem.at[1])
    q_s[...] = jnp.sum(p_r[...], axis=0) * (1.0 / math.sqrt(C4 * L**3))

    @pl.when(even)
    def _():
        remote(q_s, q_r, q_sem.at[0], q_sem.at[1], (down, sp)).start()
        arrived(q_r, q_sem.at[1])

    @pl.when(odd == 1)
    def _():
        q_r[...] = q_s[...]

    result = q_r[...]
    for q in range(4):
        rows = result if q == 0 else turn(result, K - q * ORB)
        projection[8 * q : 8 * q + 8, :] = rows[:, :ORB]

    arrived(fx_s, fx_sem.at[0])
    arrived(fy_s.at[pl.ds(0, SPACE - 1)], fy_sem.at[0])
    arrived(p_r.at[pl.ds(0, SPACE - 1)], p_sem.at[0])
    for g in range(G):
        arrived(s1.at[g, :, pl.ds(0, L - R)], s1_send.at[g])
        arrived(s2.at[g, :, pl.ds(0, L - R)], s2_send.at[g])

    @pl.when(even)
    def _():
        for g in range(G - 1):
            arrived(w_in.at[g], z_send.at[g])
        arrived(yh, f_send)
        arrived(fy_r, ff_sem.at[0])
        arrived(q_s, q_sem.at[0])

    @pl.when(odd == 1)
    def _():
        arrived(out_v, o_send)

    arrived(out_v, o_recv)


def body(blocks, fields, trial):
    diagonal, mats = tables()
    bf16, f32 = jnp.bfloat16, jnp.float32
    vmem = pl.BlockSpec(memory_space=pltpu.VMEM)
    hbm = pl.BlockSpec(memory_space=pl.ANY)
    dma = pltpu.SemaphoreType.DMA
    by_x = pltpu.VMEM((G, R, L, ZS, K), bf16)
    by_pair = pltpu.VMEM((G, L, R, ZS, K), bf16)
    one_row = pltpu.VMEM((G, L, ZS, K), bf16)
    packed = pltpu.VMEM((SPACE, 16, K), bf16)
    tile = pltpu.VMEM((8, K), f32)
    scratch = [pltpu.VMEM(fields.shape, f32)] + [pltpu.VMEM(m.shape, m.dtype) for m in mats]
    scratch += [
        by_x, by_x, pltpu.VMEM((L, R, ZS, K), bf16), by_pair, one_row, one_row, by_x, by_x, by_x, by_x,
        pltpu.VMEM((G, K, R * ROWS), bf16),
        pltpu.VMEM((2, R, L, K), bf16), pltpu.VMEM((2, R, L, K), bf16),
        packed, packed, packed,
        pltpu.VMEM((SPACE, R, TRI, 2 * K), f32), pltpu.VMEM((G, R, ROWS, 2 * K), f32),
        pltpu.VMEM((K, K), f32), tile, pltpu.VMEM((SPACE, 8, K), f32), tile, tile,
        dma((G,)), dma((G,)), dma(()), dma(()), dma((G,)), dma((G,)), dma((5,)), dma((G,)), dma((5,)), dma(()), dma(()), dma(()),
        dma((2,)), dma((2,)), dma((2,)), dma((2,)), dma((2,)), dma((10,)),
    ]
    return pl.pallas_call(
        lambda *refs: kernel(diagonal, *refs),
        out_shape=(
            jax.ShapeDtypeStruct(blocks.shape, bf16),
            jax.ShapeDtypeStruct((ORB, ORB), f32),
        ),
        in_specs=[hbm] * (3 + len(mats)),
        out_specs=(hbm, vmem),
        scratch_shapes=scratch,
        compiler_params=pltpu.CompilerParams(
            collective_id=0, has_side_effects=True, vmem_limit_bytes=56 * 1024 * 1024
        ),
    )(blocks, fields, trial, *[jnp.asarray(m) for m in mats])


def solution(mesh):
    in_specs = (
        P(("tm", "space"), None, None, None),
        P(("tm", "space"), None, None),
        P("space", None, None, None),
    )
    out_specs = (P(("tm", "space"), None, None, None), P("tm", None))
    return jax.shard_map(body, mesh=mesh, in_specs=in_specs, out_specs=out_specs, check_vma=False)
```

```python
import math

import jax
import jax.numpy as jnp
import ml_dtypes
import numpy as np
from jax import lax
from jax.experimental import pallas as pl
from jax.experimental.pallas import tpu as pltpu
from jax.sharding import PartitionSpec as P

L = 48
C4 = 4
ORB = 32
K = C4 * ORB

KINETIC = 0.0716
MIX_SCALAR = 0.25
MIX_ISOSPIN = 0.15

TM = 32
GRID = 4
SPACE = GRID * GRID
R = L // SPACE
ZS = 16
G = L // ZS
ROWS = L * ZS
TRI = G * R * ZS
MESH = pl.DeviceIdType.MESH
ONE_HOP = [(0, 1), (1, 0), (0, 3), (3, 0), (1, 1), (3, 3), (1, 3), (3, 1)]
TWO_HOPS = [
    ((0, 1), (0, 1)), ((1, 0), (1, 0)), ((1, 1), (1, 1)),
    ((0, 3), (1, 3)), ((0, 3), (3, 3)), ((3, 0), (3, 1)), ((3, 0), (3, 3)),
]


def tables():
    modes = np.arange(L) - L // 2
    damping = np.exp(-0.5 * KINETIC * (2 * math.pi / L * modes) ** 2)
    sites = np.arange(L)
    offset = sites[:, None] - sites[None, :]
    kernel = (damping[:, None, None] * np.cos(2 * math.pi / L * modes[:, None, None] * offset)).sum(0) / L
    diagonal = float(kernel[0, 0])
    unit = kernel / diagonal

    major = np.kron(unit, np.eye(ZS))
    minor = np.einsum("azbw,xy->axzbyw", unit.reshape(G, ZS, G, ZS), np.eye(R)).reshape(TRI, TRI)

    lanes = np.zeros((3 * L, 3 * K))
    for z in range(L):
        lanes[z, z] = 1
        lanes[2 * L + z, L + z] = 1
        lanes[L + z, K + z] = 1
        lanes[L + z, 2 * K + L + z] = 1
    pack = np.zeros((SPACE, 16, 3, R, L))
    for j in range(SPACE):
        for x in range(R):
            for y in range(R):
                n = x * R + y
                pack[j, n, 0, x, R * j + y] = 1
                pack[j, 9 + n // 2, 1 + n % 2, x, R * j + y] = 1
    pack = pack.reshape(SPACE * 16, 3 * R * L)
    pick = np.zeros((2, R, G, R, ZS, 16))
    keep = np.zeros((2, R, G, R, ZS, K))
    for y in range(R):
        for x in range(R):
            n = x * R + y
            pick[0, y, :, x, :, n] = 1
            pick[1, y, :, x, :, 9 + n // 2] = 1
            for g in range(G):
                for z in range(ZS):
                    keep[0, y, g, x, z, [ZS * g + z, L + ZS * g + z]] = 1
                    keep[1, y, g, x, z, L * (n % 2) + ZS * g + z] = 1
    pick = pick.reshape(2 * R * TRI, 16)
    keep = keep.reshape(2 * R * TRI, K)
    spread = np.kron(np.eye(L), np.ones((ZS, 1)))
    keep_z = np.zeros((G, ZS, 2 * K))
    for g in range(G):
        for z in range(ZS):
            keep_z[g, z, [ZS * g + z, L + ZS * g + z, K + ZS * g + z]] = 1
    fill = np.zeros((2 * K, 2 * K))
    fill[:L, :K] = 1
    fill[L : 2 * L, : K // 2] = 1
    fill[L : 2 * L, K // 2 : K] = -1
    fill[K : K + 2 * L, K:] = 1
    bf16 = lambda a: np.asarray(a, np.float32).astype(ml_dtypes.bfloat16)
    f32 = lambda a: np.asarray(a, np.float32)
    mats = [bf16(major), bf16(minor), bf16(lanes), bf16(pack), bf16(pick), f32(keep), bf16(spread), f32(keep_z), bf16(fill)]
    return diagonal, mats


def dot(a, b):
    return jnp.dot(a, b, preferred_element_type=jnp.float32)


def lanes3(parts):
    return jnp.concatenate(parts, axis=1)


def turn(value, shift):
    return pltpu.roll(value, shift, axis=1)


def kernel(
    diagonal,
    blocks, fields, trial, major_h, minor_h, lanes_h, pack_h, pick_h, keep_h, spread_h, keep_z_h, fill_h,
    handed, projection,
    fields_v, major, minor, lanes, pack, pick, keep, spread, keep_z, fill,
    w_in, s1, y1, t1, t2, s2, x2, out_v, trial_v, trial_t, st1, st1_y, st2, st2_g, fx_s, fx_r, fy_s, fy_r, fy, c1, c2,
    prod, p_s, p_r, q_s, q_r,
    z_send, z_recv, f_send, f_recv, s1_send, y1_recv, st1_recv, st1_send, st2_recv, st2_send, s2_send, x2_recv, o_send, o_recv, tr_sem,
    fx_sem, fy_sem, ff_sem, p_sem, q_sem, in_sem,
):
    bf16 = jnp.bfloat16
    tm = lax.axis_index("tm")
    sp = lax.axis_index("space")
    odd = lax.rem(tm, 2)
    even = odd == 0
    up = lax.rem(tm + 2, TM)
    down = lax.rem(tm + TM - 2, TM)
    beside = lax.rem(tm + TM - 1 + 2 * odd, TM)
    my_y = sp // GRID
    my_x = lax.rem(sp, GRID)
    cube = diagonal**3

    def peer(k):
        return lax.rem(my_y + k // GRID, GRID) * GRID + lax.rem(my_x + lax.rem(k, GRID), GRID)

    def at(offset):
        return lax.rem(my_y + offset[0], GRID) * GRID + lax.rem(my_x + offset[1], GRID)

    def remote(src, dst, send, recv, device):
        return pltpu.make_async_remote_copy(
            src_ref=src, dst_ref=dst, send_sem=send, recv_sem=recv, device_id=device, device_id_type=MESH
        )

    def to_peers(copy):
        @pl.loop(1, SPACE)
        def _(k):
            copy(peer(k))

    def exchange(source, target, stage, send, stage_sem, recv):
        for n, (first, second) in enumerate(TWO_HOPS):
            total = (first[0] + second[0], first[1] + second[1])
            remote(source(at(total)), stage.at[n], send, stage_sem, (tm, at(first))).start()
        for offset in ONE_HOP:
            remote(source(at(offset)), target(sp), send, recv, (tm, at(offset))).start()

    def forward(target, stage, stage_sem, send, recv):
        arrived(stage, stage_sem)
        for n, (first, second) in enumerate(TWO_HOPS):
            origin = at((GRID - first[0], GRID - first[1]))
            remote(stage.at[n], target(origin), send, recv, (tm, at(second))).start()

    def arrived(ref, sem):
        pltpu.make_async_copy(ref, ref, sem).wait()

    inputs = [
        pltpu.make_async_copy(src, dst, in_sem.at[n])
        for n, (src, dst) in enumerate(
            zip(
                (fields, lanes_h, pack_h, major_h, minor_h, pick_h, keep_h, spread_h, keep_z_h, fill_h),
                (fields_v, lanes, pack, major, minor, pick, keep, spread, keep_z, fill),
            )
        )
    ]
    for copy in inputs:
        copy.start()

    barrier = pltpu.get_barrier_semaphore()

    def greet(device):
        pl.semaphore_signal(barrier, inc=1, device_id=device, device_id_type=MESH)

    for other in (up, down, beside):
        greet((other, sp))
    to_peers(lambda j: greet((tm, j)))

    def own(g):
        for x in range(R):
            pltpu.make_async_copy(blocks.at[x, :, pl.ds(g * ZS, ZS), :], w_in.at[g, x], z_recv.at[g]).start()

    @pl.when(odd == 1)
    def _():
        for g in range(G - 1):
            own(g)

    own(G - 1)

    for copy in inputs:
        copy.wait()
    lane = lax.broadcasted_iota(jnp.int32, (1, 3 * L), 1)
    scale = jnp.where(lane < L, cube * MIX_SCALAR, cube * MIX_ISOSPIN)
    scaled = (fields_v[...].reshape(R * L, 3 * L) * scale).astype(bf16)
    placed = dot(scaled, lanes[...]).astype(bf16)
    fx_s[0] = placed[:, :K].reshape(R, L, K)
    fx_s[1] = placed[:, K : 2 * K].reshape(R, L, K)
    stacked = jnp.concatenate([placed[:, :K], placed[:, K : 2 * K], placed[:, 2 * K :]], axis=0)
    fy_s[...] = dot(pack[...], stacked).astype(bf16).reshape(SPACE, 16, K)
    fy_r[sp] = fy_s[sp]

    pl.semaphore_wait(barrier, SPACE + 2)

    def hand(g):
        for x in range(R):
            remote(
                blocks.at[x, :, pl.ds(g * ZS, ZS), :], w_in.at[g, x], z_send.at[g], z_recv.at[g], (up, sp)
            ).start()

    @pl.when(even)
    def _():
        hand(0)
        hand(1)

    to_peers(lambda j: remote(fy_s.at[j], fy_r.at[sp], fy_sem.at[0], fy_sem.at[1], (tm, j)).start())
    remote(fx_s, fx_r, fx_sem.at[0], fx_sem.at[1], (beside, sp)).start()

    for g in range(G):
        for x in range(R):
            pltpu.make_async_copy(trial.at[x, :, pl.ds(g * ZS, ZS), :], trial_v.at[g, x], tr_sem).start()

    @pl.when(even)
    def _():
        arrived(fy_r.at[pl.ds(0, SPACE - 1)], fy_sem.at[1])
        remote(fy_r, fy, ff_sem.at[0], ff_sem.at[1], (up, sp)).start()

    def coefficients():
        @pl.when(even)
        def _():
            arrived(fy, ff_sem.at[1])

        @pl.when(odd == 1)
        def _():
            arrived(fy_r.at[pl.ds(0, SPACE - 1)], fy_sem.at[1])
            fy[...] = fy_r[...]

        top = lax.broadcasted_iota(jnp.int32, (1, 2 * K), 1)
        constant = jnp.where(top < K, cube, 0.0)

        @pl.loop(0, SPACE)
        def _(i):
            rows = (dot(pick[...], fy[i]) * keep[...]).astype(bf16)
            both = lanes3([rows[: R * TRI], rows[R * TRI :]])
            c1[i] = (dot(both, fill[...]) + constant).reshape(R, TRI, 2 * K)

        @pl.when(odd == 1)
        def _():
            forward_rows()

        arrived(trial_v, tr_sem)

        @pl.loop(0, G)
        def _(g):
            for x in range(R):
                trial_t[g, :, x * ROWS : (x + 1) * ROWS] = jnp.transpose(trial_v[g, x].reshape(ROWS, K))

        arrived(fx_r, fx_sem.at[1])

        @pl.loop(0, R)
        def _(x):
            rows = dot(spread[...], lanes3([fx_r[0, x], fx_r[1, x]])).reshape(L, ZS, 2 * K)
            for g in range(G):
                mine = (rows * keep_z[g][None]).reshape(ROWS, 2 * K).astype(bf16)
                c2[g, x] = dot(mine, fill[...]) + constant

    def onward(y):
        remote(y1.at[G, :, y], y1.at[G - 1, :, y], f_send, f_recv.at[y], (up, sp)).start()

    def place(t):
        return jnp.where(even, lax.rem(t + G, G + 1), t)

    def forward_whole(t):
        q = place(t)
        forward(lambda i: y1.at[q, pl.ds(i * R, R)], st1.at[t], st1_recv.at[t], st1_send.at[t], y1_recv.at[q])

    def forward_rows():
        q = jnp.where(even, 1, 2)

        @pl.loop(0, R)
        def _(y):
            forward(
                lambda i: y1.at[q, pl.ds(i * R, R), y],
                st1_y.at[y], st1_recv.at[2 + y], st1_send.at[2 + y], y1_recv.at[4 + y],
            )

    @pl.loop(0, G)
    def _(t):
        g = lax.rem(t + (G - 1) * (1 - odd), G)
        q = place(t)

        @pl.when(jnp.logical_and(even, t > 0))
        def _():
            forward_whole(t - 1)

        @pl.when(jnp.logical_and(even, t == 1))
        def _():
            arrived(y1.at[G, pl.ds(0, L - R)], y1_recv.at[G])
            onward(0)

        arrived(w_in.at[g], z_recv.at[g])

        @pl.when(jnp.logical_and(even, t == G - 1))
        def _():
            onward(1)
            onward(2)

        moved = dot(major[...], lanes3([w_in[g, x].reshape(ROWS, K) for x in range(R)])).astype(bf16)
        for x in range(R):
            s1[g, x] = moved[:, x * K : (x + 1) * K].reshape(L, ZS, K)

        @pl.when(t < G - 1)
        def _():
            exchange(
                lambda j: s1.at[g, :, pl.ds(j * R, R)],
                lambda i: y1.at[q, pl.ds(i * R, R)],
                st1.at[t], s1_send.at[g], st1_recv.at[t], y1_recv.at[q],
            )

        @pl.when(t == G - 1)
        def _():
            @pl.loop(0, R)
            def _(y):
                exchange(
                    lambda j: s1.at[g, :, j * R + y],
                    lambda i: y1.at[q, pl.ds(i * R, R), y],
                    st1_y.at[y], s1_send.at[g], st1_recv.at[2 + y], y1_recv.at[4 + y],
                )

        y1[q, pl.ds(sp * R, R)] = s1[g, :, pl.ds(sp * R, R)]

        @pl.when(jnp.logical_and(odd == 1, t > 0))
        def _():
            forward_whole(t - 1)

        @pl.when(t == (G - 1) * odd)
        def _():
            coefficients()

    @pl.when(even)
    def _():
        forward_rows()

    @pl.loop(0, R)
    def _(y):
        @pl.when(y == 0)
        def _():
            arrived(y1.at[0, pl.ds(0, L - R)], y1_recv.at[0])

        @pl.when(jnp.logical_and(odd == 1, y == 0))
        def _():
            arrived(y1.at[1, pl.ds(0, L - R)], y1_recv.at[1])

        @pl.when(even)
        def _():
            arrived(y1.at[G - 1, :, y], f_recv.at[y])

        arrived(y1.at[G - 1, pl.ds(0, L - R), y], y1_recv.at[4 + y])
        moved = dot(major[...], lanes3([y1[g, :, y].reshape(ROWS, K) for g in range(G)])).astype(bf16)
        for g in range(G):
            t1[g] = moved[:, g * K : (g + 1) * K].reshape(L, ZS, K)

        def pair(n, carry):
            def column(i):
                return jnp.concatenate([t1[g, pl.ds(i * R, R)].reshape(R * ZS, K) for g in range(G)], axis=0)

            both = dot(minor[...], lanes3([column(2 * n), column(2 * n + 1)]))
            mixed = []
            for m in range(2):
                own = both[:, m * K : (m + 1) * K]
                coefs = c1[2 * n + m, y]
                mixed.append((coefs[:, :K] * own + coefs[:, K:] * turn(own, K // 2)).astype(bf16))
            again = dot(minor[...], lanes3(mixed)).astype(bf16)
            for m in range(2):
                for g in range(G):
                    t2[g, pl.ds((2 * n + m) * R, R)] = again[
                        g * R * ZS : (g + 1) * R * ZS, m * K : (m + 1) * K
                    ].reshape(R, ZS, K)
            return carry

        lax.fori_loop(0, SPACE // 2, pair, 0, unroll=4)

        moved = dot(major[...], lanes3([t2[g].reshape(ROWS, K) for g in range(G)])).astype(bf16)
        for g in range(G):
            s2[y, g] = moved[:, g * K : (g + 1) * K].reshape(L, ZS, K)

        @pl.when(y < R - 1)
        def _():
            exchange(
                lambda j: s2.at[y, :, pl.ds(j * R, R)],
                lambda i: x2.at[:, :, i * R + y],
                st2.at[y], s2_send.at[y], st2_recv.at[y], x2_recv.at[y],
            )

        @pl.when(y == R - 1)
        def _():
            @pl.loop(0, G)
            def _(g):
                exchange(
                    lambda j: s2.at[y, g, pl.ds(j * R, R)],
                    lambda i: x2.at[g, :, i * R + y],
                    st2_g.at[g], s2_send.at[y], st2_recv.at[2 + g], x2_recv.at[2 + g],
                )

        x2[:, :, sp * R + y] = s2[y, :, pl.ds(sp * R, R)]

        @pl.when(y > 0)
        def _():
            forward(
                lambda i: x2.at[:, :, i * R + y - 1],
                st2.at[y - 1], st2_recv.at[y - 1], st2_send.at[y - 1], x2_recv.at[y - 1],
            )

    @pl.loop(0, G)
    def _(g):
        forward(
            lambda i: x2.at[g, :, i * R + R - 1],
            st2_g.at[g], st2_recv.at[2 + g], st2_send.at[2 + g], x2_recv.at[2 + g],
        )

    prod[...] = jnp.zeros_like(prod)
    for y in range(R - 1):
        arrived(x2.at[:, :, pl.ds(0, SPACE - 1)], x2_recv.at[y])

    @pl.loop(0, G)
    def _(g):
        arrived(x2.at[g, :, pl.ds(0, SPACE - 1)], x2_recv.at[R - 1 + g])
        moved = dot(major[...], lanes3([x2[g, x].reshape(ROWS, K) for x in range(R)]))
        for x in range(R):
            own = moved[:, x * K : (x + 1) * K]
            coefs = c2[g, x]
            mixed = (coefs[:, :K] * own + coefs[:, K:] * turn(own, K // 2)).astype(bf16)
            out_v[g, x] = mixed.reshape(L, ZS, K)
            target = handed.at[x, :, pl.ds(g * ZS, ZS), :]

            @pl.when(even)
            def _():
                pltpu.make_async_copy(out_v.at[g, x], target, o_recv).start()

            @pl.when(odd == 1)
            def _():
                remote(out_v.at[g, x], target, o_send, o_recv, (up, sp)).start()

        prod[...] += dot(trial_t[g], out_v[g].reshape(R * ROWS, K))

    total = prod[:ORB]
    for c in range(1, C4):
        total = total + turn(prod[c * ORB : (c + 1) * ORB], K - c * ORB)
    quarter = lax.broadcasted_iota(jnp.int32, (8, K), 1) // ORB
    packed = jnp.where(quarter == 0, total[:8], 0.0)
    for q in range(1, 4):
        packed = packed + jnp.where(quarter == q, turn(total[8 * q : 8 * q + 8], q * ORB), 0.0)
    p_s[...] = packed
    p_r[sp] = packed
    to_peers(lambda j: remote(p_s, p_r.at[sp], p_sem.at[0], p_sem.at[1], (tm, j)).start())
    arrived(p_r.at[pl.ds(0, SPACE - 1)], p_sem.at[1])
    q_s[...] = jnp.sum(p_r[...], axis=0) * (1.0 / math.sqrt(C4 * L**3))

    @pl.when(even)
    def _():
        remote(q_s, q_r, q_sem.at[0], q_sem.at[1], (down, sp)).start()
        arrived(q_r, q_sem.at[1])

    @pl.when(odd == 1)
    def _():
        q_r[...] = q_s[...]

    result = q_r[...]
    for q in range(4):
        rows = result if q == 0 else turn(result, K - q * ORB)
        projection[8 * q : 8 * q + 8, :] = rows[:, :ORB]

    arrived(fx_s, fx_sem.at[0])
    arrived(fy_s.at[pl.ds(0, SPACE - 1)], fy_sem.at[0])
    arrived(p_r.at[pl.ds(0, SPACE - 1)], p_sem.at[0])
    for g in range(G):
        arrived(s1.at[g, :, pl.ds(0, L - R)], s1_send.at[g])
        arrived(s2.at[g, :, pl.ds(0, L - R)], s2_send.at[g])

    @pl.when(even)
    def _():
        for g in range(G - 1):
            arrived(w_in.at[g], z_send.at[g])
        arrived(y1.at[G], f_send)
        arrived(fy_r, ff_sem.at[0])
        arrived(q_s, q_sem.at[0])

    for t in range(2):
        arrived(st1.at[t], st1_send.at[t])
        arrived(st2.at[t], st2_send.at[t])
    for n in range(3):
        arrived(st1_y.at[n], st1_send.at[2 + n])
        arrived(st2_g.at[n], st2_send.at[2 + n])

    @pl.when(odd == 1)
    def _():
        arrived(out_v, o_send)

    arrived(out_v, o_recv)


def body(blocks, fields, trial):
    diagonal, mats = tables()
    bf16, f32 = jnp.bfloat16, jnp.float32
    vmem = pl.BlockSpec(memory_space=pltpu.VMEM)
    hbm = pl.BlockSpec(memory_space=pl.ANY)
    dma = pltpu.SemaphoreType.DMA
    by_x = pltpu.VMEM((G, R, L, ZS, K), bf16)
    one_row = pltpu.VMEM((G, L, ZS, K), bf16)
    packed = pltpu.VMEM((SPACE, 16, K), bf16)
    tile = pltpu.VMEM((8, K), f32)
    scratch = [pltpu.VMEM(fields.shape, f32)] + [pltpu.VMEM(m.shape, m.dtype) for m in mats]
    scratch += [
        by_x, by_x, pltpu.VMEM((G + 1, L, R, ZS, K), bf16), one_row, one_row, by_x, by_x, by_x, by_x,
        pltpu.VMEM((G, K, R * ROWS), bf16),
        pltpu.VMEM((2, 7, R, R, ZS, K), bf16), pltpu.VMEM((R, 7, R, ZS, K), bf16),
        pltpu.VMEM((2, 7, G, R, ZS, K), bf16), pltpu.VMEM((G, 7, R, ZS, K), bf16),
        pltpu.VMEM((2, R, L, K), bf16), pltpu.VMEM((2, R, L, K), bf16),
        packed, packed, packed,
        pltpu.VMEM((SPACE, R, TRI, 2 * K), f32), pltpu.VMEM((G, R, ROWS, 2 * K), f32),
        pltpu.VMEM((K, K), f32), tile, pltpu.VMEM((SPACE, 8, K), f32), tile, tile,
        dma((G,)), dma((G,)), dma(()), dma((G,)), dma((G,)), dma((7,)), dma((5,)), dma((5,)), dma((5,)), dma((5,)), dma((G,)), dma((5,)), dma(()), dma(()), dma(()),
        dma((2,)), dma((2,)), dma((2,)), dma((2,)), dma((2,)), dma((10,)),
    ]
    return pl.pallas_call(
        lambda *refs: kernel(diagonal, *refs),
        out_shape=(
            jax.ShapeDtypeStruct(blocks.shape, bf16),
            jax.ShapeDtypeStruct((ORB, ORB), f32),
        ),
        in_specs=[hbm] * (3 + len(mats)),
        out_specs=(hbm, vmem),
        scratch_shapes=scratch,
        compiler_params=pltpu.CompilerParams(
            collective_id=0, has_side_effects=True, vmem_limit_bytes=56 * 1024 * 1024
        ),
    )(blocks, fields, trial, *[jnp.asarray(m) for m in mats])


def solution(mesh):
    in_specs = (
        P(("tm", "space"), None, None, None),
        P(("tm", "space"), None, None),
        P("space", None, None, None),
    )
    out_specs = (P(("tm", "space"), None, None, None), P("tm", None))
    return jax.shard_map(body, mesh=mesh, in_specs=in_specs, out_specs=out_specs, check_vma=False)
```

```python
import math

import jax
import jax.numpy as jnp
import ml_dtypes
import numpy as np
from jax import lax
from jax.experimental import pallas as pl
from jax.experimental.pallas import tpu as pltpu
from jax.sharding import PartitionSpec as P

L = 48
C4 = 4
ORB = 32
K = C4 * ORB

KINETIC = 0.0716
MIX_SCALAR = 0.25
MIX_ISOSPIN = 0.15

TM = 32
GRID = 4
SPACE = GRID * GRID
R = L // SPACE
ZS = 16
G = L // ZS
ROWS = L * ZS
TRI = G * R * ZS
MESH = pl.DeviceIdType.MESH


def tables():
    modes = np.arange(L) - L // 2
    damping = np.exp(-0.5 * KINETIC * (2 * math.pi / L * modes) ** 2)
    sites = np.arange(L)
    offset = sites[:, None] - sites[None, :]
    kernel = (damping[:, None, None] * np.cos(2 * math.pi / L * modes[:, None, None] * offset)).sum(0) / L
    diagonal = float(kernel[0, 0])
    unit = kernel / diagonal

    major = np.kron(unit, np.eye(ZS))
    minor = np.einsum("azbw,xy->axzbyw", unit.reshape(G, ZS, G, ZS), np.eye(R)).reshape(TRI, TRI)

    lanes = np.zeros((3 * L, 3 * K))
    for z in range(L):
        lanes[z, z] = 1
        lanes[2 * L + z, L + z] = 1
        lanes[L + z, K + z] = 1
        lanes[L + z, 2 * K + L + z] = 1
    pack = np.zeros((SPACE, 16, 3, R, L))
    for j in range(SPACE):
        for x in range(R):
            for y in range(R):
                n = x * R + y
                pack[j, n, 0, x, R * j + y] = 1
                pack[j, 9 + n // 2, 1 + n % 2, x, R * j + y] = 1
    pack = pack.reshape(SPACE * 16, 3 * R * L)
    keep = np.zeros((3, G, ZS, K))
    for g in range(G):
        for z in range(ZS):
            keep[0, g, z, [ZS * g + z, L + ZS * g + z]] = 1
            keep[1, g, z, ZS * g + z] = 1
            keep[2, g, z, L + ZS * g + z] = 1
    spread = np.kron(np.eye(L), np.ones((ZS, 1)))
    keep_z = np.zeros((G, ZS, 2 * K))
    for g in range(G):
        for z in range(ZS):
            keep_z[g, z, [ZS * g + z, L + ZS * g + z, K + ZS * g + z]] = 1
    fill = np.zeros((2 * K, 2 * K))
    fill[:L, :K] = 1
    fill[L : 2 * L, : K // 2] = 1
    fill[L : 2 * L, K // 2 : K] = -1
    fill[K : K + 2 * L, K:] = 1
    bf16 = lambda a: np.asarray(a, np.float32).astype(ml_dtypes.bfloat16)
    f32 = lambda a: np.asarray(a, np.float32)
    mats = [bf16(major), bf16(minor), bf16(lanes), bf16(pack), f32(keep), bf16(spread), f32(keep_z), bf16(fill)]
    return diagonal, mats


def dot(a, b):
    return jnp.dot(a, b, preferred_element_type=jnp.float32)


def lanes3(parts):
    return jnp.concatenate(parts, axis=1)


def turn(value, shift):
    return pltpu.roll(value, shift, axis=1)


def kernel(
    diagonal,
    blocks, fields, trial, major_h, minor_h, lanes_h, pack_h, keep_h, spread_h, keep_z_h, fill_h,
    handed, projection,
    fields_v, major, minor, lanes, pack, keep, spread, keep_z, fill,
    w_in, s1, yh, y1, t1, t2, s2, x2, out_v, trial_v, trial_t, fx_s, fx_r, fy_s, fy_r, fy, c1, c2,
    prod, p_s, p_r, q_s, q_r,
    z_send, z_recv, h_recv, f_send, f_recv, s1_send, y1_recv, s2_send, x2_recv, o_send, o_recv, tr_sem,
    fx_sem, fy_sem, ff_sem, p_sem, q_sem, in_sem,
):
    bf16 = jnp.bfloat16
    tm = lax.axis_index("tm")
    sp = lax.axis_index("space")
    odd = lax.rem(tm, 2)
    even = odd == 0
    up = lax.rem(tm + 2, TM)
    down = lax.rem(tm + TM - 2, TM)
    beside = lax.rem(tm + TM - 1 + 2 * odd, TM)
    my_y = sp // GRID
    my_x = lax.rem(sp, GRID)
    cube = diagonal**3

    def peer(k):
        return lax.rem(my_y + k // GRID, GRID) * GRID + lax.rem(my_x + lax.rem(k, GRID), GRID)

    def remote(src, dst, send, recv, device):
        return pltpu.make_async_remote_copy(
            src_ref=src, dst_ref=dst, send_sem=send, recv_sem=recv, device_id=device, device_id_type=MESH
        )

    def to_peers(copy):
        @pl.loop(1, SPACE)
        def _(k):
            copy(peer(k))

    def arrived(ref, sem):
        pltpu.make_async_copy(ref, ref, sem).wait()

    inputs = [
        pltpu.make_async_copy(src, dst, in_sem.at[n])
        for n, (src, dst) in enumerate(
            zip(
                (fields, lanes_h, pack_h, major_h, minor_h, keep_h, spread_h, keep_z_h, fill_h),
                (fields_v, lanes, pack, major, minor, keep, spread, keep_z, fill),
            )
        )
    ]
    for copy in inputs:
        copy.start()

    barrier = pltpu.get_barrier_semaphore()

    def greet(device):
        pl.semaphore_signal(barrier, inc=1, device_id=device, device_id_type=MESH)

    for other in (up, down, beside):
        greet((other, sp))
    to_peers(lambda j: greet((tm, j)))

    def own(g):
        for x in range(R):
            pltpu.make_async_copy(blocks.at[x, :, pl.ds(g * ZS, ZS), :], w_in.at[g, x], z_recv.at[g]).start()

    @pl.when(odd == 1)
    def _():
        for g in range(G - 1):
            own(g)

    own(G - 1)

    for copy in inputs:
        copy.wait()
    lane = lax.broadcasted_iota(jnp.int32, (1, 3 * L), 1)
    scale = jnp.where(lane < L, cube * MIX_SCALAR, cube * MIX_ISOSPIN)
    scaled = (fields_v[...].reshape(R * L, 3 * L) * scale).astype(bf16)
    placed = dot(scaled, lanes[...]).astype(bf16)
    fx_s[0] = placed[:, :K].reshape(R, L, K)
    fx_s[1] = placed[:, K : 2 * K].reshape(R, L, K)
    stacked = jnp.concatenate([placed[:, :K], placed[:, K : 2 * K], placed[:, 2 * K :]], axis=0)
    fy_s[...] = dot(pack[...], stacked).astype(bf16).reshape(SPACE, 16, K)
    fy_r[sp] = fy_s[sp]

    pl.semaphore_wait(barrier, SPACE + 2)

    def hand(g):
        for x in range(R):
            remote(
                blocks.at[x, :, pl.ds(g * ZS, ZS), :], w_in.at[g, x], z_send.at[g], z_recv.at[g], (up, sp)
            ).start()

    @pl.when(even)
    def _():
        hand(0)
        hand(1)

    to_peers(lambda j: remote(fy_s.at[j], fy_r.at[sp], fy_sem.at[0], fy_sem.at[1], (tm, j)).start())
    remote(fx_s, fx_r, fx_sem.at[0], fx_sem.at[1], (beside, sp)).start()

    for g in range(G):
        for x in range(R):
            pltpu.make_async_copy(trial.at[x, :, pl.ds(g * ZS, ZS), :], trial_v.at[g, x], tr_sem).start()

    @pl.when(even)
    def _():
        arrived(fy_r.at[pl.ds(0, SPACE - 1)], fy_sem.at[1])
        remote(fy_r, fy, ff_sem.at[0], ff_sem.at[1], (up, sp)).start()

    top = lax.broadcasted_iota(jnp.int32, (1, 2 * K), 1)
    constant = jnp.where(top < K, cube, 0.0)

    def first_coefficients():
        @pl.when(even)
        def _():
            arrived(fy, ff_sem.at[1])

        @pl.when(odd == 1)
        def _():
            arrived(fy_r.at[pl.ds(0, SPACE - 1)], fy_sem.at[1])
            fy[...] = fy_r[...]

        def one(i, carry):
            rows = fy[i].astype(jnp.float32)
            both = []
            for y in range(R):
                diagonal_part, flip_part = [], []
                for g in range(G):
                    for x in range(R):
                        n = x * R + y
                        diagonal_part.append(rows[n : n + 1] * keep[0, g])
                        flip_part.append(rows[9 + n // 2 : 10 + n // 2] * keep[1 + n % 2, g])
                both.append(lanes3([jnp.concatenate(part, axis=0) for part in (diagonal_part, flip_part)]))
            picked = jnp.concatenate(both, axis=0).astype(bf16)
            c1[i] = (dot(picked, fill[...]) + constant).reshape(R, TRI, 2 * K)
            return carry

        lax.fori_loop(0, SPACE, one, 0, unroll=2)

    def second_coefficients():
        arrived(fx_r, fx_sem.at[1])

        @pl.loop(0, R)
        def _(x):
            rows = dot(spread[...], lanes3([fx_r[0, x], fx_r[1, x]])).reshape(L, ZS, 2 * K)
            for g in range(G):
                mine = (rows * keep_z[g][None]).reshape(ROWS, 2 * K).astype(bf16)
                c2[g, x] = dot(mine, fill[...]) + constant

    def turn_trial():
        arrived(trial_v, tr_sem)

        @pl.loop(0, G)
        def _(g):
            for x in range(R):
                trial_t[g, :, x * ROWS : (x + 1) * ROWS] = jnp.transpose(trial_v[g, x].reshape(ROWS, K))

    def products(g):
        prod[...] += dot(trial_t[g], out_v[g].reshape(R * ROWS, K))

    def onward(y):
        remote(yh.at[:, y], y1.at[G - 1, :, y], f_send, f_recv.at[y], (up, sp)).start()

    @pl.loop(0, G)
    def _(t):
        g = lax.rem(t + (G - 1) * (1 - odd), G)
        arrived(w_in.at[g], z_recv.at[g])

        @pl.when(jnp.logical_and(even, t == G - 1))
        def _():
            onward(1)
            onward(2)

        moved = dot(major[...], lanes3([w_in[g, x].reshape(ROWS, K) for x in range(R)])).astype(bf16)
        for x in range(R):
            s1[g, x] = moved[:, x * K : (x + 1) * K].reshape(L, ZS, K)

        home = jnp.logical_and(even, t == 0)

        @pl.when(home)
        def _():
            to_peers(
                lambda j: remote(
                    s1.at[g, :, pl.ds(j * R, R)], yh.at[pl.ds(sp * R, R)], s1_send.at[g], h_recv, (tm, j)
                ).start()
            )
            yh[pl.ds(sp * R, R)] = s1[g, :, pl.ds(sp * R, R)]

        @pl.when(jnp.logical_not(home))
        def _():
            @pl.when(t < G - 1)
            def _():
                to_peers(
                    lambda j: remote(
                        s1.at[g, :, pl.ds(j * R, R)], y1.at[g, pl.ds(sp * R, R)], s1_send.at[g], y1_recv.at[g], (tm, j)
                    ).start()
                )

            @pl.when(t == G - 1)
            def _():
                for y in range(R):
                    to_peers(
                        lambda j: remote(
                            s1.at[g, :, j * R + y],
                            y1.at[g, pl.ds(sp * R, R), y],
                            s1_send.at[g],
                            y1_recv.at[G - 1 + y],
                            (tm, j),
                        ).start()
                    )

            y1[g, pl.ds(sp * R, R)] = s1[g, :, pl.ds(sp * R, R)]

        @pl.when(home)
        def _():
            turn_trial()

        @pl.when(t == 1 + odd)
        def _():
            first_coefficients()

        @pl.when(jnp.logical_and(even, t == 1))
        def _():
            arrived(yh.at[pl.ds(0, L - R)], h_recv)
            onward(0)

    @pl.loop(0, R)
    def _(y):
        @pl.when(y == 0)
        def _():
            arrived(y1.at[0, pl.ds(0, L - R)], y1_recv.at[0])

        @pl.when(jnp.logical_and(odd == 1, y == 0))
        def _():
            arrived(y1.at[1, pl.ds(0, L - R)], y1_recv.at[1])

        @pl.when(even)
        def _():
            arrived(y1.at[G - 1, :, y], f_recv.at[y])

        arrived(y1.at[G - 1, pl.ds(0, L - R), y], y1_recv.at[G - 1 + y])
        moved = dot(major[...], lanes3([y1[g, :, y].reshape(ROWS, K) for g in range(G)])).astype(bf16)
        for g in range(G):
            t1[g] = moved[:, g * K : (g + 1) * K].reshape(L, ZS, K)

        def pair(n, carry):
            def column(i):
                return jnp.concatenate([t1[g, pl.ds(i * R, R)].reshape(R * ZS, K) for g in range(G)], axis=0)

            both = dot(minor[...], lanes3([column(2 * n), column(2 * n + 1)]))
            mixed = []
            for m in range(2):
                own = both[:, m * K : (m + 1) * K]
                coefs = c1[2 * n + m, y]
                mixed.append((coefs[:, :K] * own + coefs[:, K:] * turn(own, K // 2)).astype(bf16))
            again = dot(minor[...], lanes3(mixed)).astype(bf16)
            for m in range(2):
                for g in range(G):
                    t2[g, pl.ds((2 * n + m) * R, R)] = again[
                        g * R * ZS : (g + 1) * R * ZS, m * K : (m + 1) * K
                    ].reshape(R, ZS, K)
            return carry

        lax.fori_loop(0, SPACE // 2, pair, 0, unroll=4)

        moved = dot(major[...], lanes3([t2[g].reshape(ROWS, K) for g in range(G)])).astype(bf16)
        for g in range(G):
            s2[y, g] = moved[:, g * K : (g + 1) * K].reshape(L, ZS, K)

        @pl.when(y < R - 1)
        def _():
            to_peers(
                lambda j: remote(
                    s2.at[y, :, pl.ds(j * R, R)], x2.at[:, :, sp * R + y], s2_send.at[y], x2_recv.at[y], (tm, j)
                ).start()
            )

        @pl.when(y == R - 1)
        def _():
            for g in range(G):
                to_peers(
                    lambda j: remote(
                        s2.at[y, g, pl.ds(j * R, R)], x2.at[g, :, sp * R + y], s2_send.at[y], x2_recv.at[y + g], (tm, j)
                    ).start()
                )

        x2[:, :, sp * R + y] = s2[y, :, pl.ds(sp * R, R)]

    second_coefficients()
    prod[...] = jnp.zeros_like(prod)
    for y in range(R - 1):
        arrived(x2.at[:, :, pl.ds(0, SPACE - 1)], x2_recv.at[y])

    @pl.loop(0, G)
    def _(g):
        arrived(x2.at[g, :, pl.ds(0, SPACE - 1)], x2_recv.at[R - 1 + g])
        moved = dot(major[...], lanes3([x2[g, x].reshape(ROWS, K) for x in range(R)]))
        for x in range(R):
            own = moved[:, x * K : (x + 1) * K]
            coefs = c2[g, x]
            mixed = (coefs[:, :K] * own + coefs[:, K:] * turn(own, K // 2)).astype(bf16)
            out_v[g, x] = mixed.reshape(L, ZS, K)
            target = handed.at[x, :, pl.ds(g * ZS, ZS), :]

            @pl.when(even)
            def _():
                pltpu.make_async_copy(out_v.at[g, x], target, o_recv).start()

            @pl.when(odd == 1)
            def _():
                remote(out_v.at[g, x], target, o_send, o_recv, (up, sp)).start()

        @pl.when(even)
        def _():
            products(g)

    @pl.when(odd == 1)
    def _():
        turn_trial()
        for g in range(G):
            products(g)

    total = prod[:ORB]
    for c in range(1, C4):
        total = total + turn(prod[c * ORB : (c + 1) * ORB], K - c * ORB)
    quarter = lax.broadcasted_iota(jnp.int32, (8, K), 1) // ORB
    packed = jnp.where(quarter == 0, total[:8], 0.0)
    for q in range(1, 4):
        packed = packed + jnp.where(quarter == q, turn(total[8 * q : 8 * q + 8], q * ORB), 0.0)
    p_s[...] = packed
    p_r[sp] = packed
    to_peers(lambda j: remote(p_s, p_r.at[sp], p_sem.at[0], p_sem.at[1], (tm, j)).start())
    arrived(p_r.at[pl.ds(0, SPACE - 1)], p_sem.at[1])
    q_s[...] = jnp.sum(p_r[...], axis=0) * (1.0 / math.sqrt(C4 * L**3))

    @pl.when(even)
    def _():
        remote(q_s, q_r, q_sem.at[0], q_sem.at[1], (down, sp)).start()
        arrived(q_r, q_sem.at[1])

    @pl.when(odd == 1)
    def _():
        q_r[...] = q_s[...]

    result = q_r[...]
    for q in range(4):
        rows = result if q == 0 else turn(result, K - q * ORB)
        projection[8 * q : 8 * q + 8, :] = rows[:, :ORB]

    arrived(fx_s, fx_sem.at[0])
    arrived(fy_s.at[pl.ds(0, SPACE - 1)], fy_sem.at[0])
    arrived(p_r.at[pl.ds(0, SPACE - 1)], p_sem.at[0])
    for g in range(G):
        arrived(s1.at[g, :, pl.ds(0, L - R)], s1_send.at[g])
        arrived(s2.at[g, :, pl.ds(0, L - R)], s2_send.at[g])

    @pl.when(even)
    def _():
        for g in range(G - 1):
            arrived(w_in.at[g], z_send.at[g])
        arrived(yh, f_send)
        arrived(fy_r, ff_sem.at[0])
        arrived(q_s, q_sem.at[0])

    @pl.when(odd == 1)
    def _():
        arrived(out_v, o_send)

    arrived(out_v, o_recv)


def body(blocks, fields, trial):
    diagonal, mats = tables()
    bf16, f32 = jnp.bfloat16, jnp.float32
    vmem = pl.BlockSpec(memory_space=pltpu.VMEM)
    hbm = pl.BlockSpec(memory_space=pl.ANY)
    dma = pltpu.SemaphoreType.DMA
    by_x = pltpu.VMEM((G, R, L, ZS, K), bf16)
    by_pair = pltpu.VMEM((G, L, R, ZS, K), bf16)
    one_row = pltpu.VMEM((G, L, ZS, K), bf16)
    packed = pltpu.VMEM((SPACE, 16, K), bf16)
    tile = pltpu.VMEM((8, K), f32)
    scratch = [pltpu.VMEM(fields.shape, f32)] + [pltpu.VMEM(m.shape, m.dtype) for m in mats]
    scratch += [
        by_x, by_x, pltpu.VMEM((L, R, ZS, K), bf16), by_pair, one_row, one_row, by_x, by_x, by_x, by_x,
        pltpu.VMEM((G, K, R * ROWS), bf16),
        pltpu.VMEM((2, R, L, K), bf16), pltpu.VMEM((2, R, L, K), bf16),
        packed, packed, packed,
        pltpu.VMEM((SPACE, R, TRI, 2 * K), f32), pltpu.VMEM((G, R, ROWS, 2 * K), f32),
        pltpu.VMEM((K, K), f32), tile, pltpu.VMEM((SPACE, 8, K), f32), tile, tile,
        dma((G,)), dma((G,)), dma(()), dma(()), dma((G,)), dma((G,)), dma((5,)), dma((G,)), dma((5,)), dma(()), dma(()), dma(()),
        dma((2,)), dma((2,)), dma((2,)), dma((2,)), dma((2,)), dma((9,)),
    ]
    return pl.pallas_call(
        lambda *refs: kernel(diagonal, *refs),
        out_shape=(
            jax.ShapeDtypeStruct(blocks.shape, bf16),
            jax.ShapeDtypeStruct((ORB, ORB), f32),
        ),
        in_specs=[hbm] * (3 + len(mats)),
        out_specs=(hbm, vmem),
        scratch_shapes=scratch,
        compiler_params=pltpu.CompilerParams(
            collective_id=0, has_side_effects=True, vmem_limit_bytes=56 * 1024 * 1024
        ),
    )(blocks, fields, trial, *[jnp.asarray(m) for m in mats])


def solution(mesh):
    in_specs = (
        P(("tm", "space"), None, None, None),
        P(("tm", "space"), None, None),
        P("space", None, None, None),
    )
    out_specs = (P(("tm", "space"), None, None, None), P("tm", None))
    return jax.shard_map(body, mesh=mesh, in_specs=in_specs, out_specs=out_specs, check_vma=False)
```

```python
import math

import jax
import jax.numpy as jnp
import ml_dtypes
import numpy as np
from jax import lax
from jax.experimental import pallas as pl
from jax.experimental.pallas import tpu as pltpu
from jax.sharding import PartitionSpec as P

L = 48
C4 = 4
ORB = 32
K = C4 * ORB

KINETIC = 0.0716
MIX_SCALAR = 0.25
MIX_ISOSPIN = 0.15

TM = 32
GRID = 4
SPACE = GRID * GRID
R = L // SPACE
ZS = 16
G = L // ZS
ROWS = L * ZS
TRI = G * R * ZS
MESH = pl.DeviceIdType.MESH


def tables():
    modes = np.arange(L) - L // 2
    damping = np.exp(-0.5 * KINETIC * (2 * math.pi / L * modes) ** 2)
    sites = np.arange(L)
    offset = sites[:, None] - sites[None, :]
    kernel = (damping[:, None, None] * np.cos(2 * math.pi / L * modes[:, None, None] * offset)).sum(0) / L
    diagonal = float(kernel[0, 0])
    unit = kernel / diagonal

    major = np.kron(unit, np.eye(ZS))
    minor = np.einsum("azbw,xy->axzbyw", unit.reshape(G, ZS, G, ZS), np.eye(R)).reshape(TRI, TRI)

    lanes = np.zeros((3 * L, 3 * K))
    for z in range(L):
        lanes[z, z] = 1
        lanes[2 * L + z, L + z] = 1
        lanes[L + z, K + z] = 1
        lanes[L + z, 2 * K + L + z] = 1
    pack = np.zeros((SPACE, 16, 3, R, L))
    for j in range(SPACE):
        for x in range(R):
            for y in range(R):
                n = x * R + y
                pack[j, n, 0, x, R * j + y] = 1
                pack[j, 9 + n // 2, 1 + n % 2, x, R * j + y] = 1
    pack = pack.reshape(SPACE * 16, 3 * R * L)
    keep = np.zeros((3, G, ZS, K))
    for g in range(G):
        for z in range(ZS):
            keep[0, g, z, [ZS * g + z, L + ZS * g + z]] = 1
            keep[1, g, z, ZS * g + z] = 1
            keep[2, g, z, L + ZS * g + z] = 1
    spread = np.kron(np.eye(L), np.ones((ZS, 1)))
    keep_z = np.zeros((G, ZS, 2 * K))
    for g in range(G):
        for z in range(ZS):
            keep_z[g, z, [ZS * g + z, L + ZS * g + z, K + ZS * g + z]] = 1
    fill = np.zeros((2 * K, 2 * K))
    fill[:L, :K] = 1
    fill[L : 2 * L, : K // 2] = 1
    fill[L : 2 * L, K // 2 : K] = -1
    fill[K : K + 2 * L, K:] = 1
    bf16 = lambda a: np.asarray(a, np.float32).astype(ml_dtypes.bfloat16)
    f32 = lambda a: np.asarray(a, np.float32)
    mats = [bf16(major), bf16(minor), bf16(lanes), bf16(pack), f32(keep), bf16(spread), f32(keep_z), bf16(fill)]
    return diagonal, mats


def dot(a, b):
    return jnp.dot(a, b, preferred_element_type=jnp.float32)


def lanes3(parts):
    return jnp.concatenate(parts, axis=1)


def turn(value, shift):
    return pltpu.roll(value, shift, axis=1)


def kernel(
    diagonal,
    blocks, fields, trial, major_h, minor_h, lanes_h, pack_h, keep_h, spread_h, keep_z_h, fill_h,
    handed, projection,
    fields_v, major, minor, lanes, pack, keep, spread, keep_z, fill,
    w_in, s1, yh, y1, t1, t2, s2, x2, out_v, trial_v, trial_t, fx_s, fx_r, fy_s, fy_r, fy, c1, c2,
    prod, p_s, p_r,
    z_send, z_recv, h_recv, f_send, f_recv, s1_send, y1_recv, s2_send, x2_recv, o_send, o_recv, tr_sem,
    fx_sem, fy_sem, ff_sem, p_sem, in_sem,
):
    bf16 = jnp.bfloat16
    tm = lax.axis_index("tm")
    sp = lax.axis_index("space")
    odd = lax.rem(tm, 2)
    even = odd == 0
    up = lax.rem(tm + 2, TM)
    down = lax.rem(tm + TM - 2, TM)
    beside = lax.rem(tm + TM - 1 + 2 * odd, TM)
    my_y = sp // GRID
    my_x = lax.rem(sp, GRID)
    cube = diagonal**3

    def peer(k):
        return lax.rem(my_y + k // GRID, GRID) * GRID + lax.rem(my_x + k % GRID, GRID)

    def remote(src, dst, send, recv, device):
        return pltpu.make_async_remote_copy(
            src_ref=src, dst_ref=dst, send_sem=send, recv_sem=recv, device_id=device, device_id_type=MESH
        )

    peers = [peer(k) for k in range(1, SPACE)]

    def to_peers(copy):
        for j in peers:
            copy(j)

    def arrived(ref, sem):
        pltpu.make_async_copy(ref, ref, sem).wait()

    inputs = [
        pltpu.make_async_copy(src, dst, in_sem.at[n])
        for n, (src, dst) in enumerate(
            zip(
                (fields, lanes_h, pack_h, major_h, minor_h, keep_h, spread_h, keep_z_h, fill_h),
                (fields_v, lanes, pack, major, minor, keep, spread, keep_z, fill),
            )
        )
    ]
    for copy in inputs:
        copy.start()

    barrier = pltpu.get_barrier_semaphore()

    def greet(device):
        pl.semaphore_signal(barrier, inc=1, device_id=device, device_id_type=MESH)

    greet((beside, sp))
    to_peers(lambda j: greet((tm, j)))

    @pl.when(even)
    def _():
        for j in range(SPACE):
            greet((up, j))
            greet((down, j))

    @pl.when(odd == 1)
    def _():
        greet((up, sp))
        greet((down, sp))

    def own(g):
        for x in range(R):
            pltpu.make_async_copy(blocks.at[x, :, pl.ds(g * ZS, ZS), :], w_in.at[g, x], z_recv.at[g]).start()

    @pl.when(odd == 1)
    def _():
        for g in range(G - 1):
            own(g)

    own(G - 1)

    pl.semaphore_wait(barrier, SPACE + 2 + 2 * (SPACE - 1) * (1 - odd))

    def hand(g):
        for x in range(R):
            remote(
                blocks.at[x, :, pl.ds(g * ZS, ZS), :], w_in.at[g, x], z_send.at[g], z_recv.at[g], (up, sp)
            ).start()

    @pl.when(even)
    def _():
        hand(0)
        hand(1)

    for g in range(G):
        for x in range(R):
            pltpu.make_async_copy(trial.at[x, :, pl.ds(g * ZS, ZS), :], trial_v.at[g, x], tr_sem).start()

    for copy in inputs:
        copy.wait()

    def share_fields():
        lane = lax.broadcasted_iota(jnp.int32, (1, 3 * L), 1)
        scale = jnp.where(lane < L, cube * MIX_SCALAR, cube * MIX_ISOSPIN)
        scaled = (fields_v[...].reshape(R * L, 3 * L) * scale).astype(bf16)
        placed = dot(scaled, lanes[...]).astype(bf16)
        fx_s[0] = placed[:, :K].reshape(R, L, K)
        fx_s[1] = placed[:, K : 2 * K].reshape(R, L, K)
        stacked = jnp.concatenate([placed[:, :K], placed[:, K : 2 * K], placed[:, 2 * K :]], axis=0)
        fy_s[...] = dot(pack[...], stacked).astype(bf16).reshape(SPACE, 16, K)
        fy_r[sp] = fy_s[sp]
        to_peers(lambda j: remote(fy_s.at[j], fy_r.at[sp], fy_sem.at[0], fy_sem.at[1], (tm, j)).start())
        remote(fx_s, fx_r, fx_sem.at[0], fx_sem.at[1], (beside, sp)).start()

    def hand_fields():
        arrived(fy_r.at[pl.ds(0, SPACE - 1)], fy_sem.at[1])
        remote(fy_r, fy, ff_sem.at[0], ff_sem.at[1], (up, sp)).start()

    top = lax.broadcasted_iota(jnp.int32, (1, 2 * K), 1)
    constant = jnp.where(top < K, cube, 0.0)

    def first_coefficients():
        @pl.when(even)
        def _():
            arrived(fy, ff_sem.at[1])

        @pl.when(odd == 1)
        def _():
            arrived(fy_r.at[pl.ds(0, SPACE - 1)], fy_sem.at[1])
            fy[...] = fy_r[...]

        def one(i, carry):
            rows = fy[i].astype(jnp.float32)
            both = []
            for y in range(R):
                diagonal_part, flip_part = [], []
                for g in range(G):
                    for x in range(R):
                        n = x * R + y
                        diagonal_part.append(rows[n : n + 1] * keep[0, g])
                        flip_part.append(rows[9 + n // 2 : 10 + n // 2] * keep[1 + n % 2, g])
                both.append(lanes3([jnp.concatenate(part, axis=0) for part in (diagonal_part, flip_part)]))
            picked = jnp.concatenate(both, axis=0).astype(bf16)
            c1[i] = (dot(picked, fill[...]) + constant).reshape(R, TRI, 2 * K)
            return carry

        lax.fori_loop(0, SPACE, one, 0, unroll=2)

    def second_coefficients():
        arrived(fx_r, fx_sem.at[1])

        @pl.loop(0, R)
        def _(x):
            rows = dot(spread[...], lanes3([fx_r[0, x], fx_r[1, x]])).reshape(L, ZS, 2 * K)
            for g in range(G):
                mine = (rows * keep_z[g][None]).reshape(ROWS, 2 * K).astype(bf16)
                c2[g, x] = dot(mine, fill[...]) + constant

    def turn_trial():
        arrived(trial_v, tr_sem)

        @pl.loop(0, G)
        def _(g):
            for x in range(R):
                trial_t[g, :, x * ROWS : (x + 1) * ROWS] = jnp.transpose(trial_v[g, x].reshape(ROWS, K))

    def products(g):
        prod[...] += dot(trial_t[g], out_v[g].reshape(R * ROWS, K))

    def onward(y):
        remote(yh.at[:, y], y1.at[G - 1, :, y], f_send, f_recv.at[y], (up, sp)).start()

    @pl.loop(0, G)
    def _(t):
        g = lax.rem(t + (G - 1) * (1 - odd), G)
        arrived(w_in.at[g], z_recv.at[g])

        @pl.when(jnp.logical_and(even, t == G - 1))
        def _():
            onward(1)
            onward(2)

        moved = dot(major[...], lanes3([w_in[g, x].reshape(ROWS, K) for x in range(R)])).astype(bf16)
        for x in range(R):
            s1[g, x] = moved[:, x * K : (x + 1) * K].reshape(L, ZS, K)

        home = jnp.logical_and(even, t == 0)

        @pl.when(home)
        def _():
            to_peers(
                lambda j: remote(
                    s1.at[g, :, pl.ds(j * R, R)], yh.at[pl.ds(sp * R, R)], s1_send.at[g], h_recv, (tm, j)
                ).start()
            )
            yh[pl.ds(sp * R, R)] = s1[g, :, pl.ds(sp * R, R)]

        @pl.when(jnp.logical_not(home))
        def _():
            @pl.when(t < G - 1)
            def _():
                to_peers(
                    lambda j: remote(
                        s1.at[g, :, pl.ds(j * R, R)], y1.at[g, pl.ds(sp * R, R)], s1_send.at[g], y1_recv.at[g], (tm, j)
                    ).start()
                )

            @pl.when(t == G - 1)
            def _():
                for y in range(R):
                    to_peers(
                        lambda j: remote(
                            s1.at[g, :, j * R + y],
                            y1.at[g, pl.ds(sp * R, R), y],
                            s1_send.at[g],
                            y1_recv.at[G - 1 + y],
                            (tm, j),
                        ).start()
                    )

            y1[g, pl.ds(sp * R, R)] = s1[g, :, pl.ds(sp * R, R)]

        @pl.when(t == 0)
        def _():
            share_fields()

        @pl.when(home)
        def _():
            turn_trial()
            hand_fields()

        @pl.when(t == 1 + odd)
        def _():
            first_coefficients()

        @pl.when(jnp.logical_and(even, t == 1))
        def _():
            arrived(yh.at[pl.ds(0, L - R)], h_recv)
            onward(0)

    @pl.loop(0, R)
    def _(y):
        @pl.when(y == 0)
        def _():
            arrived(y1.at[0, pl.ds(0, L - R)], y1_recv.at[0])

        @pl.when(jnp.logical_and(odd == 1, y == 0))
        def _():
            arrived(y1.at[1, pl.ds(0, L - R)], y1_recv.at[1])

        @pl.when(even)
        def _():
            arrived(y1.at[G - 1, :, y], f_recv.at[y])

        arrived(y1.at[G - 1, pl.ds(0, L - R), y], y1_recv.at[G - 1 + y])
        moved = dot(major[...], lanes3([y1[g, :, y].reshape(ROWS, K) for g in range(G)])).astype(bf16)
        for g in range(G):
            t1[g] = moved[:, g * K : (g + 1) * K].reshape(L, ZS, K)

        def pair(n, carry):
            def column(i):
                return jnp.concatenate([t1[g, pl.ds(i * R, R)].reshape(R * ZS, K) for g in range(G)], axis=0)

            both = dot(minor[...], lanes3([column(2 * n), column(2 * n + 1)]))
            mixed = []
            for m in range(2):
                own = both[:, m * K : (m + 1) * K]
                coefs = c1[2 * n + m, y]
                mixed.append((coefs[:, :K] * own + coefs[:, K:] * turn(own, K // 2)).astype(bf16))
            again = dot(minor[...], lanes3(mixed)).astype(bf16)
            for m in range(2):
                for g in range(G):
                    t2[g, pl.ds((2 * n + m) * R, R)] = again[
                        g * R * ZS : (g + 1) * R * ZS, m * K : (m + 1) * K
                    ].reshape(R, ZS, K)
            return carry

        lax.fori_loop(0, SPACE // 2, pair, 0, unroll=4)

        moved = dot(major[...], lanes3([t2[g].reshape(ROWS, K) for g in range(G)])).astype(bf16)
        for g in range(G):
            s2[y, g] = moved[:, g * K : (g + 1) * K].reshape(L, ZS, K)

        @pl.when(y < R - 1)
        def _():
            to_peers(
                lambda j: remote(
                    s2.at[y, :, pl.ds(j * R, R)], x2.at[:, :, sp * R + y], s2_send.at[y], x2_recv.at[y], (tm, j)
                ).start()
            )

        @pl.when(y == R - 1)
        def _():
            for g in range(G):
                to_peers(
                    lambda j: remote(
                        s2.at[y, g, pl.ds(j * R, R)], x2.at[g, :, sp * R + y], s2_send.at[y], x2_recv.at[y + g], (tm, j)
                    ).start()
                )

        x2[:, :, sp * R + y] = s2[y, :, pl.ds(sp * R, R)]

    second_coefficients()
    prod[...] = jnp.zeros_like(prod)
    for y in range(R - 1):
        arrived(x2.at[:, :, pl.ds(0, SPACE - 1)], x2_recv.at[y])

    @pl.loop(0, G)
    def _(g):
        arrived(x2.at[g, :, pl.ds(0, SPACE - 1)], x2_recv.at[R - 1 + g])
        moved = dot(major[...], lanes3([x2[g, x].reshape(ROWS, K) for x in range(R)]))
        for x in range(R):
            own = moved[:, x * K : (x + 1) * K]
            coefs = c2[g, x]
            mixed = (coefs[:, :K] * own + coefs[:, K:] * turn(own, K // 2)).astype(bf16)
            out_v[g, x] = mixed.reshape(L, ZS, K)
            target = handed.at[x, :, pl.ds(g * ZS, ZS), :]

            @pl.when(even)
            def _():
                pltpu.make_async_copy(out_v.at[g, x], target, o_recv).start()

            @pl.when(odd == 1)
            def _():
                remote(out_v.at[g, x], target, o_send, o_recv, (up, sp)).start()

        @pl.when(even)
        def _():
            products(g)

    @pl.when(odd == 1)
    def _():
        turn_trial()
        for g in range(G):
            products(g)

    total = prod[:ORB]
    for c in range(1, C4):
        total = total + turn(prod[c * ORB : (c + 1) * ORB], K - c * ORB)
    quarter = lax.broadcasted_iota(jnp.int32, (8, K), 1) // ORB
    packed = jnp.where(quarter == 0, total[:8], 0.0)
    for q in range(1, 4):
        packed = packed + jnp.where(quarter == q, turn(total[8 * q : 8 * q + 8], q * ORB), 0.0)
    p_s[...] = packed

    @pl.when(even)
    def _():
        for j in range(SPACE):
            remote(p_s, p_r.at[sp], p_sem.at[0], p_sem.at[1], (down, j)).start()
        arrived(p_r, p_sem.at[1])

    @pl.when(odd == 1)
    def _():
        p_r[sp] = packed
        to_peers(lambda j: remote(p_s, p_r.at[sp], p_sem.at[0], p_sem.at[1], (tm, j)).start())
        arrived(p_r.at[pl.ds(0, SPACE - 1)], p_sem.at[1])

    result = jnp.sum(p_r[...], axis=0) * (1.0 / math.sqrt(C4 * L**3))
    for q in range(4):
        rows = result if q == 0 else turn(result, K - q * ORB)
        projection[8 * q : 8 * q + 8, :] = rows[:, :ORB]

    arrived(fx_s, fx_sem.at[0])
    arrived(fy_s.at[pl.ds(0, SPACE - 1)], fy_sem.at[0])
    for g in range(G):
        arrived(s1.at[g, :, pl.ds(0, L - R)], s1_send.at[g])
        arrived(s2.at[g, :, pl.ds(0, L - R)], s2_send.at[g])

    @pl.when(even)
    def _():
        for g in range(G - 1):
            arrived(w_in.at[g], z_send.at[g])
        arrived(yh, f_send)
        arrived(fy_r, ff_sem.at[0])
        arrived(p_r, p_sem.at[0])

    @pl.when(odd == 1)
    def _():
        arrived(out_v, o_send)
        arrived(p_r.at[pl.ds(0, SPACE - 1)], p_sem.at[0])

    arrived(out_v, o_recv)


def leave(handed, projection, handed_out, projection_out, held, in_sems, out_sems):
    places = [(x, pl.ds(n * (L // 2), L // 2)) for x in range(R) for n in range(2)]
    reads = [pltpu.make_async_copy(handed.at[p], held.at[p], in_sems.at[n]) for n, p in enumerate(places)]
    writes = [pltpu.make_async_copy(held.at[p], handed_out.at[p], out_sems.at[n]) for n, p in enumerate(places)]
    for copy in reads:
        copy.start()
    projection_out[...] = projection[...]
    for read, write in zip(reads, writes):
        read.wait()
        write.start()
    for copy in writes:
        copy.wait()


def body(blocks, fields, trial):
    diagonal, mats = tables()
    bf16, f32 = jnp.bfloat16, jnp.float32
    vmem = pl.BlockSpec(memory_space=pltpu.VMEM)
    hbm = pl.BlockSpec(memory_space=pl.ANY)
    dma = pltpu.SemaphoreType.DMA
    by_x = pltpu.VMEM((G, R, L, ZS, K), bf16)
    by_pair = pltpu.VMEM((G, L, R, ZS, K), bf16)
    one_row = pltpu.VMEM((G, L, ZS, K), bf16)
    packed = pltpu.VMEM((SPACE, 16, K), bf16)
    tile = pltpu.VMEM((8, K), f32)
    scratch = [pltpu.VMEM(fields.shape, f32)] + [pltpu.VMEM(m.shape, m.dtype) for m in mats]
    scratch += [
        by_x, by_x, pltpu.VMEM((L, R, ZS, K), bf16), by_pair, one_row, one_row, by_x, by_x, by_x, by_x,
        pltpu.VMEM((G, K, R * ROWS), bf16),
        pltpu.VMEM((2, R, L, K), bf16), pltpu.VMEM((2, R, L, K), bf16),
        packed, packed, packed,
        pltpu.VMEM((SPACE, R, TRI, 2 * K), f32), pltpu.VMEM((G, R, ROWS, 2 * K), f32),
        pltpu.VMEM((K, K), f32), tile, pltpu.VMEM((SPACE, 8, K), f32),
        dma((G,)), dma((G,)), dma(()), dma(()), dma((G,)), dma((G,)), dma((5,)), dma((G,)), dma((5,)), dma(()), dma(()), dma(()),
        dma((2,)), dma((2,)), dma((2,)), dma((2,)), dma((9,)),
    ]
    shapes = (jax.ShapeDtypeStruct(blocks.shape, bf16), jax.ShapeDtypeStruct((ORB, ORB), f32))
    results = pl.pallas_call(
        lambda *refs: kernel(diagonal, *refs),
        out_shape=shapes,
        in_specs=[hbm] * (3 + len(mats)),
        out_specs=(hbm, vmem),
        scratch_shapes=scratch,
        compiler_params=pltpu.CompilerParams(
            collective_id=0, has_side_effects=True, vmem_limit_bytes=56 * 1024 * 1024
        ),
    )(blocks, fields, trial, *[jnp.asarray(m) for m in mats])
    return pl.pallas_call(
        leave,
        out_shape=shapes,
        in_specs=[hbm, vmem],
        out_specs=(hbm, vmem),
        scratch_shapes=[pltpu.VMEM(blocks.shape, bf16), dma((2 * R,)), dma((2 * R,))],
    )(*results)


def solution(mesh):
    in_specs = (
        P(("tm", "space"), None, None, None),
        P(("tm", "space"), None, None),
        P("space", None, None, None),
    )
    out_specs = (P(("tm", "space"), None, None, None), P("tm", None))
    return jax.shard_map(body, mesh=mesh, in_specs=in_specs, out_specs=out_specs, check_vma=False)
```

```python
import math

import jax
import jax.numpy as jnp
import ml_dtypes
import numpy as np
from jax import lax
from jax.experimental import pallas as pl
from jax.experimental.pallas import tpu as pltpu
from jax.sharding import PartitionSpec as P

L = 48
C4 = 4
ORB = 32
K = C4 * ORB

KINETIC = 0.0716
MIX_SCALAR = 0.25
MIX_ISOSPIN = 0.15

TM = 32
GRID = 4
SPACE = GRID * GRID
R = L // SPACE
ZS = 16
G = L // ZS
ROWS = L * ZS
TRI = G * R * ZS
MESH = pl.DeviceIdType.MESH


def tables():
    modes = np.arange(L) - L // 2
    damping = np.exp(-0.5 * KINETIC * (2 * math.pi / L * modes) ** 2)
    sites = np.arange(L)
    offset = sites[:, None] - sites[None, :]
    kernel = (damping[:, None, None] * np.cos(2 * math.pi / L * modes[:, None, None] * offset)).sum(0) / L
    diagonal = float(kernel[0, 0])
    unit = kernel / diagonal

    major = np.kron(unit, np.eye(ZS))
    minor = np.einsum("azbw,xy->axzbyw", unit.reshape(G, ZS, G, ZS), np.eye(R)).reshape(TRI, TRI)

    lanes = np.zeros((3 * L, 3 * K))
    for z in range(L):
        lanes[z, z] = 1
        lanes[2 * L + z, L + z] = 1
        lanes[L + z, K + z] = 1
        lanes[L + z, 2 * K + L + z] = 1
    pack = np.zeros((SPACE, 16, 3, R, L))
    for j in range(SPACE):
        for x in range(R):
            for y in range(R):
                n = x * R + y
                pack[j, n, 0, x, R * j + y] = 1
                pack[j, 9 + n // 2, 1 + n % 2, x, R * j + y] = 1
    pack = pack.reshape(SPACE * 16, 3 * R * L)
    keep = np.zeros((3, G, ZS, K))
    for g in range(G):
        for z in range(ZS):
            keep[0, g, z, [ZS * g + z, L + ZS * g + z]] = 1
            keep[1, g, z, ZS * g + z] = 1
            keep[2, g, z, L + ZS * g + z] = 1
    spread = np.kron(np.eye(L), np.ones((ZS, 1)))
    keep_z = np.zeros((G, ZS, 2 * K))
    for g in range(G):
        for z in range(ZS):
            keep_z[g, z, [ZS * g + z, L + ZS * g + z, K + ZS * g + z]] = 1
    fill = np.zeros((2 * K, 2 * K))
    fill[:L, :K] = 1
    fill[L : 2 * L, : K // 2] = 1
    fill[L : 2 * L, K // 2 : K] = -1
    fill[K : K + 2 * L, K:] = 1
    bf16 = lambda a: np.asarray(a, np.float32).astype(ml_dtypes.bfloat16)
    f32 = lambda a: np.asarray(a, np.float32)
    mats = [bf16(major), bf16(minor), bf16(lanes), bf16(pack), f32(keep), bf16(spread), f32(keep_z), bf16(fill)]
    return diagonal, mats


def dot(a, b):
    return jnp.dot(a, b, preferred_element_type=jnp.float32)


def lanes3(parts):
    return jnp.concatenate(parts, axis=1)


def turn(value, shift):
    return pltpu.roll(value, shift, axis=1)


def kernel(
    diagonal,
    blocks, fields, trial, major_h, minor_h, lanes_h, pack_h, keep_h, spread_h, keep_z_h, fill_h,
    handed, projection,
    fields_v, major, minor, lanes, pack, keep, spread, keep_z, fill,
    w_in, s1, yh, y1, t1, t2, s2, s3, x2, out_v, trial_v, trial_t, fx_s, fx_r, fy_s, fy_r, fy, c1, c2,
    prod, p_s, p_r,
    z_send, z_recv, h_recv, f_send, f_recv, s1_send, y1_recv, s2_send, x2_recv, m_send, m_recv, o_recv, tr_sem,
    fx_sem, fy_sem, ff_sem, p_sem, in_sem,
):
    bf16 = jnp.bfloat16
    tm = lax.axis_index("tm")
    sp = lax.axis_index("space")
    odd = lax.rem(tm, 2)
    even = odd == 0
    up = lax.rem(tm + 2, TM)
    down = lax.rem(tm + TM - 2, TM)
    after = lax.rem(tm + 1, TM)
    before = lax.rem(tm + TM - 1, TM)
    my_y = sp // GRID
    my_x = lax.rem(sp, GRID)
    cube = diagonal**3

    def peer(k):
        return lax.rem(my_y + k // GRID, GRID) * GRID + lax.rem(my_x + k % GRID, GRID)

    def remote(src, dst, send, recv, device):
        return pltpu.make_async_remote_copy(
            src_ref=src, dst_ref=dst, send_sem=send, recv_sem=recv, device_id=device, device_id_type=MESH
        )

    peers = [peer(k) for k in range(1, SPACE)]

    def to_peers(copy):
        for j in peers:
            copy(j)

    def arrived(ref, sem):
        pltpu.make_async_copy(ref, ref, sem).wait()

    inputs = [
        pltpu.make_async_copy(src, dst, in_sem.at[n])
        for n, (src, dst) in enumerate(
            zip(
                (fields, lanes_h, pack_h, major_h, minor_h, keep_h, spread_h, keep_z_h, fill_h),
                (fields_v, lanes, pack, major, minor, keep, spread, keep_z, fill),
            )
        )
    ]
    for copy in inputs:
        copy.start()

    barrier = pltpu.get_barrier_semaphore()

    def greet(device):
        pl.semaphore_signal(barrier, inc=1, device_id=device, device_id_type=MESH)

    greet((after, sp))
    greet((before, sp))
    to_peers(lambda j: greet((tm, j)))
    for j in range(SPACE):
        greet((up, j))
        greet((down, j))

    def own(g):
        for x in range(R):
            pltpu.make_async_copy(blocks.at[x, :, pl.ds(g * ZS, ZS), :], w_in.at[g, x], z_recv.at[g]).start()

    @pl.when(odd == 1)
    def _():
        for g in range(G - 1):
            own(g)

    own(G - 1)

    pl.semaphore_wait(barrier, 3 * SPACE + 1)

    def hand(g):
        for x in range(R):
            remote(
                blocks.at[x, :, pl.ds(g * ZS, ZS), :], w_in.at[g, x], z_send.at[g], z_recv.at[g], (up, sp)
            ).start()

    @pl.when(even)
    def _():
        hand(0)
        hand(1)

    for g in range(G):
        for x in range(R):
            pltpu.make_async_copy(trial.at[x, :, pl.ds(g * ZS, ZS), :], trial_v.at[g, x], tr_sem).start()

    for copy in inputs:
        copy.wait()

    def share_fields():
        lane = lax.broadcasted_iota(jnp.int32, (1, 3 * L), 1)
        scale = jnp.where(lane < L, cube * MIX_SCALAR, cube * MIX_ISOSPIN)
        scaled = (fields_v[...].reshape(R * L, 3 * L) * scale).astype(bf16)
        placed = dot(scaled, lanes[...]).astype(bf16)
        fx_s[0] = placed[:, :K].reshape(R, L, K)
        fx_s[1] = placed[:, K : 2 * K].reshape(R, L, K)
        stacked = jnp.concatenate([placed[:, :K], placed[:, K : 2 * K], placed[:, 2 * K :]], axis=0)
        fy_s[...] = dot(pack[...], stacked).astype(bf16).reshape(SPACE, 16, K)
        fy_r[sp] = fy_s[sp]
        to_peers(lambda j: remote(fy_s.at[j], fy_r.at[sp], fy_sem.at[0], fy_sem.at[1], (tm, j)).start())
        remote(fx_s, fx_r, fx_sem.at[0], fx_sem.at[1], (after, sp)).start()

    def hand_fields():
        arrived(fy_r.at[pl.ds(0, SPACE - 1)], fy_sem.at[1])
        remote(fy_r, fy, ff_sem.at[0], ff_sem.at[1], (up, sp)).start()

    top = lax.broadcasted_iota(jnp.int32, (1, 2 * K), 1)
    constant = jnp.where(top < K, cube, 0.0)

    def first_coefficients():
        @pl.when(even)
        def _():
            arrived(fy, ff_sem.at[1])

        @pl.when(odd == 1)
        def _():
            arrived(fy_r.at[pl.ds(0, SPACE - 1)], fy_sem.at[1])
            fy[...] = fy_r[...]

        def one(i, carry):
            rows = fy[i].astype(jnp.float32)
            both = []
            for y in range(R):
                diagonal_part, flip_part = [], []
                for g in range(G):
                    for x in range(R):
                        n = x * R + y
                        diagonal_part.append(rows[n : n + 1] * keep[0, g])
                        flip_part.append(rows[9 + n // 2 : 10 + n // 2] * keep[1 + n % 2, g])
                both.append(lanes3([jnp.concatenate(part, axis=0) for part in (diagonal_part, flip_part)]))
            picked = jnp.concatenate(both, axis=0).astype(bf16)
            c1[i] = (dot(picked, fill[...]) + constant).reshape(R, TRI, 2 * K)
            return carry

        lax.fori_loop(0, SPACE, one, 0, unroll=2)

    def second_coefficients():
        arrived(fx_r, fx_sem.at[1])

        @pl.loop(0, R)
        def _(x):
            rows = dot(spread[...], lanes3([fx_r[0, x], fx_r[1, x]])).reshape(L, ZS, 2 * K)
            for g in range(G):
                mine = (rows * keep_z[g][None]).reshape(ROWS, 2 * K).astype(bf16)
                c2[g, x] = dot(mine, fill[...]) + constant

    def turn_trial():
        arrived(trial_v, tr_sem)

        @pl.loop(0, G)
        def _(g):
            for x in range(R):
                trial_t[g, :, x * ROWS : (x + 1) * ROWS] = jnp.transpose(trial_v[g, x].reshape(ROWS, K))

    def products(g):
        prod[...] += dot(trial_t[g], out_v[g].reshape(R * ROWS, K))

    def onward(y):
        remote(yh.at[:, y], y1.at[G - 1, :, y], f_send, f_recv.at[y], (up, sp)).start()

    @pl.loop(0, G)
    def _(t):
        g = lax.rem(t + (G - 1) * (1 - odd), G)
        arrived(w_in.at[g], z_recv.at[g])

        @pl.when(jnp.logical_and(even, t == G - 1))
        def _():
            onward(1)
            onward(2)

        moved = dot(major[...], lanes3([w_in[g, x].reshape(ROWS, K) for x in range(R)])).astype(bf16)
        for x in range(R):
            s1[g, x] = moved[:, x * K : (x + 1) * K].reshape(L, ZS, K)

        home = jnp.logical_and(even, t == 0)

        @pl.when(home)
        def _():
            to_peers(
                lambda j: remote(
                    s1.at[g, :, pl.ds(j * R, R)], yh.at[pl.ds(sp * R, R)], s1_send.at[g], h_recv, (tm, j)
                ).start()
            )
            yh[pl.ds(sp * R, R)] = s1[g, :, pl.ds(sp * R, R)]

        @pl.when(jnp.logical_not(home))
        def _():
            @pl.when(t < G - 1)
            def _():
                to_peers(
                    lambda j: remote(
                        s1.at[g, :, pl.ds(j * R, R)], y1.at[g, pl.ds(sp * R, R)], s1_send.at[g], y1_recv.at[g], (tm, j)
                    ).start()
                )

            @pl.when(t == G - 1)
            def _():
                for y in range(R):
                    to_peers(
                        lambda j: remote(
                            s1.at[g, :, j * R + y],
                            y1.at[g, pl.ds(sp * R, R), y],
                            s1_send.at[g],
                            y1_recv.at[G - 1 + y],
                            (tm, j),
                        ).start()
                    )

            y1[g, pl.ds(sp * R, R)] = s1[g, :, pl.ds(sp * R, R)]

        @pl.when(t == 0)
        def _():
            share_fields()

        @pl.when(home)
        def _():
            turn_trial()
            hand_fields()

        @pl.when(t == 1 + odd)
        def _():
            first_coefficients()

        @pl.when(jnp.logical_and(even, t == 1))
        def _():
            arrived(yh.at[pl.ds(0, L - R)], h_recv)
            onward(0)

    def back(rows, y):
        @pl.when(y < R - 1)
        def _():
            to_peers(
                lambda j: remote(
                    rows.at[y, :, pl.ds(j * R, R)], x2.at[:, :, sp * R + y], s2_send.at[y], x2_recv.at[y], (tm, j)
                ).start()
            )

        @pl.when(y == R - 1)
        def _():
            for g in range(G):
                to_peers(
                    lambda j: remote(
                        rows.at[y, g, pl.ds(j * R, R)], x2.at[g, :, sp * R + y], s2_send.at[y], x2_recv.at[y + g], (tm, j)
                    ).start()
                )

        x2[:, :, sp * R + y] = rows[y, :, pl.ds(sp * R, R)]

    @pl.loop(0, R)
    def _(y):
        @pl.when(y == 0)
        def _():
            arrived(y1.at[0, pl.ds(0, L - R)], y1_recv.at[0])

        @pl.when(jnp.logical_and(odd == 1, y == 0))
        def _():
            arrived(y1.at[1, pl.ds(0, L - R)], y1_recv.at[1])

        @pl.when(even)
        def _():
            arrived(y1.at[G - 1, :, y], f_recv.at[y])

        arrived(y1.at[G - 1, pl.ds(0, L - R), y], y1_recv.at[G - 1 + y])
        moved = dot(major[...], lanes3([y1[g, :, y].reshape(ROWS, K) for g in range(G)])).astype(bf16)
        for g in range(G):
            t1[g] = moved[:, g * K : (g + 1) * K].reshape(L, ZS, K)

        def pair(n, carry):
            def column(i):
                return jnp.concatenate([t1[g, pl.ds(i * R, R)].reshape(R * ZS, K) for g in range(G)], axis=0)

            both = dot(minor[...], lanes3([column(2 * n), column(2 * n + 1)]))
            mixed = []
            for m in range(2):
                own = both[:, m * K : (m + 1) * K]
                coefs = c1[2 * n + m, y]
                mixed.append((coefs[:, :K] * own + coefs[:, K:] * turn(own, K // 2)).astype(bf16))
            again = dot(minor[...], lanes3(mixed)).astype(bf16)
            for m in range(2):
                for g in range(G):
                    t2[g, pl.ds((2 * n + m) * R, R)] = again[
                        g * R * ZS : (g + 1) * R * ZS, m * K : (m + 1) * K
                    ].reshape(R, ZS, K)
            return carry

        lax.fori_loop(0, SPACE // 2, pair, 0, unroll=4)

        moved = dot(major[...], lanes3([t2[g].reshape(ROWS, K) for g in range(G)])).astype(bf16)
        for g in range(G):
            s2[y, g] = moved[:, g * K : (g + 1) * K].reshape(L, ZS, K)

        @pl.when(even)
        def _():
            back(s2, y)

        @pl.when(odd == 1)
        def _():
            remote(s2.at[y], s3.at[y], m_send.at[y], m_recv.at[y], (up, sp)).start()

            @pl.when(y > 0)
            def _():
                arrived(s3.at[y - 1], m_recv.at[y - 1])
                back(s3, y - 1)

    @pl.when(odd == 1)
    def _():
        turn_trial()
        arrived(s3.at[R - 1], m_recv.at[R - 1])
        back(s3, R - 1)

    second_coefficients()
    prod[...] = jnp.zeros_like(prod)
    for y in range(R - 1):
        arrived(x2.at[:, :, pl.ds(0, SPACE - 1)], x2_recv.at[y])

    @pl.loop(0, G)
    def _(g):
        arrived(x2.at[g, :, pl.ds(0, SPACE - 1)], x2_recv.at[R - 1 + g])
        moved = dot(major[...], lanes3([x2[g, x].reshape(ROWS, K) for x in range(R)]))
        for x in range(R):
            own = moved[:, x * K : (x + 1) * K]
            coefs = c2[g, x]
            mixed = (coefs[:, :K] * own + coefs[:, K:] * turn(own, K // 2)).astype(bf16)
            out_v[g, x] = mixed.reshape(L, ZS, K)
            target = handed.at[x, :, pl.ds(g * ZS, ZS), :]

            pltpu.make_async_copy(out_v.at[g, x], target, o_recv).start()

        products(g)

    total = prod[:ORB]
    for c in range(1, C4):
        total = total + turn(prod[c * ORB : (c + 1) * ORB], K - c * ORB)
    quarter = lax.broadcasted_iota(jnp.int32, (8, K), 1) // ORB
    packed = jnp.where(quarter == 0, total[:8], 0.0)
    for q in range(1, 4):
        packed = packed + jnp.where(quarter == q, turn(total[8 * q : 8 * q + 8], q * ORB), 0.0)
    p_s[...] = packed

    for j in range(SPACE):
        remote(p_s, p_r.at[sp], p_sem.at[0], p_sem.at[1], (down, j)).start()
    arrived(p_r, p_sem.at[1])
    result = jnp.sum(p_r[...], axis=0) * (1.0 / math.sqrt(C4 * L**3))
    for q in range(4):
        rows = result if q == 0 else turn(result, K - q * ORB)
        projection[8 * q : 8 * q + 8, :] = rows[:, :ORB]

    arrived(fx_s, fx_sem.at[0])
    arrived(p_r, p_sem.at[0])
    arrived(fy_s.at[pl.ds(0, SPACE - 1)], fy_sem.at[0])
    for g in range(G):
        arrived(s1.at[g, :, pl.ds(0, L - R)], s1_send.at[g])
        arrived(s2.at[g, :, pl.ds(0, L - R)], s2_send.at[g])

    @pl.when(even)
    def _():
        for g in range(G - 1):
            arrived(w_in.at[g], z_send.at[g])
        arrived(yh, f_send)
        arrived(fy_r, ff_sem.at[0])

    @pl.when(odd == 1)
    def _():
        for y in range(R):
            arrived(s2.at[y], m_send.at[y])

    arrived(out_v, o_recv)


def leave(handed, projection, handed_out, projection_out, held, in_sems, out_sems):
    places = [(x, pl.ds(n * (L // 2), L // 2)) for x in range(R) for n in range(2)]
    reads = [pltpu.make_async_copy(handed.at[p], held.at[p], in_sems.at[n]) for n, p in enumerate(places)]
    writes = [pltpu.make_async_copy(held.at[p], handed_out.at[p], out_sems.at[n]) for n, p in enumerate(places)]
    for copy in reads:
        copy.start()
    projection_out[...] = projection[...]
    for read, write in zip(reads, writes):
        read.wait()
        write.start()
    for copy in writes:
        copy.wait()


def body(blocks, fields, trial):
    diagonal, mats = tables()
    bf16, f32 = jnp.bfloat16, jnp.float32
    vmem = pl.BlockSpec(memory_space=pltpu.VMEM)
    hbm = pl.BlockSpec(memory_space=pl.ANY)
    dma = pltpu.SemaphoreType.DMA
    by_x = pltpu.VMEM((G, R, L, ZS, K), bf16)
    by_pair = pltpu.VMEM((G, L, R, ZS, K), bf16)
    one_row = pltpu.VMEM((G, L, ZS, K), bf16)
    packed = pltpu.VMEM((SPACE, 16, K), bf16)
    tile = pltpu.VMEM((8, K), f32)
    scratch = [pltpu.VMEM(fields.shape, f32)] + [pltpu.VMEM(m.shape, m.dtype) for m in mats]
    scratch += [
        by_x, by_x, pltpu.VMEM((L, R, ZS, K), bf16), by_pair, one_row, one_row, by_x, by_x, by_x, by_x, by_x,
        pltpu.VMEM((G, K, R * ROWS), bf16),
        pltpu.VMEM((2, R, L, K), bf16), pltpu.VMEM((2, R, L, K), bf16),
        packed, packed, packed,
        pltpu.VMEM((SPACE, R, TRI, 2 * K), f32), pltpu.VMEM((G, R, ROWS, 2 * K), f32),
        pltpu.VMEM((K, K), f32), tile, pltpu.VMEM((SPACE, 8, K), f32),
        dma((G,)), dma((G,)), dma(()), dma(()), dma((G,)), dma((G,)), dma((5,)), dma((G,)), dma((5,)), dma((R,)), dma((R,)), dma(()), dma(()),
        dma((2,)), dma((2,)), dma((2,)), dma((2,)), dma((9,)),
    ]
    shapes = (jax.ShapeDtypeStruct(blocks.shape, bf16), jax.ShapeDtypeStruct((ORB, ORB), f32))
    results = pl.pallas_call(
        lambda *refs: kernel(diagonal, *refs),
        out_shape=shapes,
        in_specs=[hbm] * (3 + len(mats)),
        out_specs=(hbm, vmem),
        scratch_shapes=scratch,
        compiler_params=pltpu.CompilerParams(
            collective_id=0, has_side_effects=True, vmem_limit_bytes=56 * 1024 * 1024
        ),
    )(blocks, fields, trial, *[jnp.asarray(m) for m in mats])
    return pl.pallas_call(
        leave,
        out_shape=shapes,
        in_specs=[hbm, vmem],
        out_specs=(hbm, vmem),
        scratch_shapes=[pltpu.VMEM(blocks.shape, bf16), dma((2 * R,)), dma((2 * R,))],
    )(*results)


def solution(mesh):
    in_specs = (
        P(("tm", "space"), None, None, None),
        P(("tm", "space"), None, None),
        P("space", None, None, None),
    )
    out_specs = (P(("tm", "space"), None, None, None), P("tm", None))
    return jax.shard_map(body, mesh=mesh, in_specs=in_specs, out_specs=out_specs, check_vma=False)
```

```python
import math

import jax
import jax.numpy as jnp
import ml_dtypes
import numpy as np
from jax import lax
from jax.experimental import pallas as pl
from jax.experimental.pallas import tpu as pltpu
from jax.sharding import PartitionSpec as P

L = 48
C4 = 4
ORB = 32
K = C4 * ORB

KINETIC = 0.0716
MIX_SCALAR = 0.25
MIX_ISOSPIN = 0.15

TM = 32
GRID = 4
SPACE = GRID * GRID
R = L // SPACE
ZS = 16
G = L // ZS
ROWS = L * ZS
TRI = G * R * ZS
MESH = pl.DeviceIdType.MESH


def tables():
    modes = np.arange(L) - L // 2
    damping = np.exp(-0.5 * KINETIC * (2 * math.pi / L * modes) ** 2)
    sites = np.arange(L)
    offset = sites[:, None] - sites[None, :]
    kernel = (damping[:, None, None] * np.cos(2 * math.pi / L * modes[:, None, None] * offset)).sum(0) / L
    diagonal = float(kernel[0, 0])
    unit = kernel / diagonal

    major = np.kron(unit, np.eye(ZS))
    minor = np.einsum("azbw,xy->axzbyw", unit.reshape(G, ZS, G, ZS), np.eye(R)).reshape(TRI, TRI)

    lanes = np.zeros((3 * L, 3 * K))
    for z in range(L):
        lanes[z, z] = 1
        lanes[2 * L + z, L + z] = 1
        lanes[L + z, K + z] = 1
        lanes[L + z, 2 * K + L + z] = 1
    pack = np.zeros((SPACE, 16, 3, R, L))
    for j in range(SPACE):
        for x in range(R):
            for y in range(R):
                n = x * R + y
                pack[j, n, 0, x, R * j + y] = 1
                pack[j, 9 + n // 2, 1 + n % 2, x, R * j + y] = 1
    pack = pack.reshape(SPACE * 16, 3 * R * L)
    keep = np.zeros((3, G, ZS, K))
    for g in range(G):
        for z in range(ZS):
            keep[0, g, z, [ZS * g + z, L + ZS * g + z]] = 1
            keep[1, g, z, ZS * g + z] = 1
            keep[2, g, z, L + ZS * g + z] = 1
    spread = np.kron(np.eye(L), np.ones((ZS, 1)))
    keep_z = np.zeros((G, ZS, 2 * K))
    for g in range(G):
        for z in range(ZS):
            keep_z[g, z, [ZS * g + z, L + ZS * g + z, K + ZS * g + z]] = 1
    fill = np.zeros((2 * K, 2 * K))
    fill[:L, :K] = 1
    fill[L : 2 * L, : K // 2] = 1
    fill[L : 2 * L, K // 2 : K] = -1
    fill[K : K + 2 * L, K:] = 1
    bf16 = lambda a: np.asarray(a, np.float32).astype(ml_dtypes.bfloat16)
    f32 = lambda a: np.asarray(a, np.float32)
    mats = [bf16(major), bf16(minor), bf16(lanes), bf16(pack), f32(keep), bf16(spread), f32(keep_z), bf16(fill)]
    return diagonal, mats


def dot(a, b):
    return jnp.dot(a, b, preferred_element_type=jnp.float32)


def lanes3(parts):
    return jnp.concatenate(parts, axis=1)


def turn(value, shift):
    return pltpu.roll(value, shift, axis=1)


def kernel(
    diagonal,
    blocks, fields, trial, major_h, minor_h, lanes_h, pack_h, keep_h, spread_h, keep_z_h, fill_h,
    handed, projection,
    fields_v, major, minor, lanes, pack, keep, spread, keep_z, fill,
    w_in, s1, yh, y1, t1, t2, s2, x2, out_v, trial_v, trial_t, fx_s, fx_r, fy_s, fy_r, fy, c1, c2,
    prod, p_s, p_r,
    z_send, z_recv, h_recv, f_send, f_recv, s1_send, y1_recv, s2_send, x2_recv, o_send, o_recv, tr_sem,
    fx_sem, fy_sem, ff_sem, p_sem, in_sem,
):
    bf16 = jnp.bfloat16
    tm = lax.axis_index("tm")
    sp = lax.axis_index("space")
    odd = lax.rem(tm, 2)
    even = odd == 0
    up = lax.rem(tm + 2, TM)
    down = lax.rem(tm + TM - 2, TM)
    beside = lax.rem(tm + TM - 1 + 2 * odd, TM)
    my_y = sp // GRID
    my_x = lax.rem(sp, GRID)
    cube = diagonal**3

    def peer(k):
        return lax.rem(my_y + k // GRID, GRID) * GRID + lax.rem(my_x + lax.rem(k, GRID), GRID)

    def remote(src, dst, send, recv, device):
        return pltpu.make_async_remote_copy(
            src_ref=src, dst_ref=dst, send_sem=send, recv_sem=recv, device_id=device, device_id_type=MESH
        )

    def to_peers(copy):
        @pl.loop(1, SPACE)
        def _(k):
            copy(peer(k))

    def arrived(ref, sem):
        pltpu.make_async_copy(ref, ref, sem).wait()

    inputs = [
        pltpu.make_async_copy(src, dst, in_sem.at[n])
        for n, (src, dst) in enumerate(
            zip(
                (fields, lanes_h, pack_h, major_h, minor_h, keep_h, spread_h, keep_z_h, fill_h),
                (fields_v, lanes, pack, major, minor, keep, spread, keep_z, fill),
            )
        )
    ]
    for copy in inputs:
        copy.start()

    barrier = pltpu.get_barrier_semaphore()

    def greet(device):
        pl.semaphore_signal(barrier, inc=1, device_id=device, device_id_type=MESH)

    greet((beside, sp))
    to_peers(lambda j: greet((tm, j)))

    @pl.when(even)
    def _():
        @pl.loop(0, SPACE)
        def _(j):
            greet((up, j))
            greet((down, j))

    @pl.when(odd == 1)
    def _():
        greet((up, sp))
        greet((down, sp))

    def own(g):
        for x in range(R):
            pltpu.make_async_copy(blocks.at[x, :, pl.ds(g * ZS, ZS), :], w_in.at[g, x], z_recv.at[g]).start()

    @pl.when(odd == 1)
    def _():
        for g in range(G - 1):
            own(g)

    own(G - 1)

    for copy in inputs:
        copy.wait()
    lane = lax.broadcasted_iota(jnp.int32, (1, 3 * L), 1)
    scale = jnp.where(lane < L, cube * MIX_SCALAR, cube * MIX_ISOSPIN)
    scaled = (fields_v[...].reshape(R * L, 3 * L) * scale).astype(bf16)
    placed = dot(scaled, lanes[...]).astype(bf16)
    fx_s[0] = placed[:, :K].reshape(R, L, K)
    fx_s[1] = placed[:, K : 2 * K].reshape(R, L, K)
    stacked = jnp.concatenate([placed[:, :K], placed[:, K : 2 * K], placed[:, 2 * K :]], axis=0)
    fy_s[...] = dot(pack[...], stacked).astype(bf16).reshape(SPACE, 16, K)
    fy_r[sp] = fy_s[sp]

    pl.semaphore_wait(barrier, SPACE + 2 + 2 * (SPACE - 1) * (1 - odd))

    def hand(g):
        for x in range(R):
            remote(
                blocks.at[x, :, pl.ds(g * ZS, ZS), :], w_in.at[g, x], z_send.at[g], z_recv.at[g], (up, sp)
            ).start()

    @pl.when(even)
    def _():
        hand(0)
        hand(1)

    to_peers(lambda j: remote(fy_s.at[j], fy_r.at[sp], fy_sem.at[0], fy_sem.at[1], (tm, j)).start())
    remote(fx_s, fx_r, fx_sem.at[0], fx_sem.at[1], (beside, sp)).start()

    for g in range(G):
        for x in range(R):
            pltpu.make_async_copy(trial.at[x, :, pl.ds(g * ZS, ZS), :], trial_v.at[g, x], tr_sem).start()

    @pl.when(even)
    def _():
        arrived(fy_r.at[pl.ds(0, SPACE - 1)], fy_sem.at[1])
        remote(fy_r, fy, ff_sem.at[0], ff_sem.at[1], (up, sp)).start()

    top = lax.broadcasted_iota(jnp.int32, (1, 2 * K), 1)
    constant = jnp.where(top < K, cube, 0.0)

    def first_coefficients():
        @pl.when(even)
        def _():
            arrived(fy, ff_sem.at[1])

        @pl.when(odd == 1)
        def _():
            arrived(fy_r.at[pl.ds(0, SPACE - 1)], fy_sem.at[1])
            fy[...] = fy_r[...]

        def one(i, carry):
            rows = fy[i].astype(jnp.float32)
            both = []
            for y in range(R):
                diagonal_part, flip_part = [], []
                for g in range(G):
                    for x in range(R):
                        n = x * R + y
                        diagonal_part.append(rows[n : n + 1] * keep[0, g])
                        flip_part.append(rows[9 + n // 2 : 10 + n // 2] * keep[1 + n % 2, g])
                both.append(lanes3([jnp.concatenate(part, axis=0) for part in (diagonal_part, flip_part)]))
            picked = jnp.concatenate(both, axis=0).astype(bf16)
            c1[i] = (dot(picked, fill[...]) + constant).reshape(R, TRI, 2 * K)
            return carry

        lax.fori_loop(0, SPACE, one, 0, unroll=2)

    def second_coefficients():
        arrived(fx_r, fx_sem.at[1])

        @pl.loop(0, R)
        def _(x):
            rows = dot(spread[...], lanes3([fx_r[0, x], fx_r[1, x]])).reshape(L, ZS, 2 * K)
            for g in range(G):
                mine = (rows * keep_z[g][None]).reshape(ROWS, 2 * K).astype(bf16)
                c2[g, x] = dot(mine, fill[...]) + constant

    def turn_trial():
        arrived(trial_v, tr_sem)

        @pl.loop(0, G)
        def _(g):
            for x in range(R):
                trial_t[g, :, x * ROWS : (x + 1) * ROWS] = jnp.transpose(trial_v[g, x].reshape(ROWS, K))

    def products(g):
        prod[...] += dot(trial_t[g], out_v[g].reshape(R * ROWS, K))

    def onward(y):
        remote(yh.at[:, y], y1.at[G - 1, :, y], f_send, f_recv.at[y], (up, sp)).start()

    @pl.loop(0, G)
    def _(t):
        g = lax.rem(t + (G - 1) * (1 - odd), G)
        arrived(w_in.at[g], z_recv.at[g])

        @pl.when(jnp.logical_and(even, t == G - 1))
        def _():
            onward(1)
            onward(2)

        moved = dot(major[...], lanes3([w_in[g, x].reshape(ROWS, K) for x in range(R)])).astype(bf16)
        for x in range(R):
            s1[g, x] = moved[:, x * K : (x + 1) * K].reshape(L, ZS, K)

        home = jnp.logical_and(even, t == 0)

        @pl.when(home)
        def _():
            to_peers(
                lambda j: remote(
                    s1.at[g, :, pl.ds(j * R, R)], yh.at[pl.ds(sp * R, R)], s1_send.at[g], h_recv, (tm, j)
                ).start()
            )
            yh[pl.ds(sp * R, R)] = s1[g, :, pl.ds(sp * R, R)]

        @pl.when(jnp.logical_not(home))
        def _():
            @pl.when(t < G - 1)
            def _():
                to_peers(
                    lambda j: remote(
                        s1.at[g, :, pl.ds(j * R, R)], y1.at[g, pl.ds(sp * R, R)], s1_send.at[g], y1_recv.at[g], (tm, j)
                    ).start()
                )

            @pl.when(t == G - 1)
            def _():
                for y in range(R):
                    to_peers(
                        lambda j: remote(
                            s1.at[g, :, j * R + y],
                            y1.at[g, pl.ds(sp * R, R), y],
                            s1_send.at[g],
                            y1_recv.at[G - 1 + y],
                            (tm, j),
                        ).start()
                    )

            y1[g, pl.ds(sp * R, R)] = s1[g, :, pl.ds(sp * R, R)]

        @pl.when(home)
        def _():
            turn_trial()

        @pl.when(t == 1 + odd)
        def _():
            first_coefficients()

        @pl.when(jnp.logical_and(even, t == 1))
        def _():
            arrived(yh.at[pl.ds(0, L - R)], h_recv)
            onward(0)

    @pl.loop(0, R)
    def _(y):
        @pl.when(y == 0)
        def _():
            arrived(y1.at[0, pl.ds(0, L - R)], y1_recv.at[0])

        @pl.when(jnp.logical_and(odd == 1, y == 0))
        def _():
            arrived(y1.at[1, pl.ds(0, L - R)], y1_recv.at[1])

        @pl.when(even)
        def _():
            arrived(y1.at[G - 1, :, y], f_recv.at[y])

        arrived(y1.at[G - 1, pl.ds(0, L - R), y], y1_recv.at[G - 1 + y])
        moved = dot(major[...], lanes3([y1[g, :, y].reshape(ROWS, K) for g in range(G)])).astype(bf16)
        for g in range(G):
            t1[g] = moved[:, g * K : (g + 1) * K].reshape(L, ZS, K)

        def pair(n, carry):
            def column(i):
                return jnp.concatenate([t1[g, pl.ds(i * R, R)].reshape(R * ZS, K) for g in range(G)], axis=0)

            both = dot(minor[...], lanes3([column(2 * n), column(2 * n + 1)]))
            mixed = []
            for m in range(2):
                own = both[:, m * K : (m + 1) * K]
                coefs = c1[2 * n + m, y]
                mixed.append((coefs[:, :K] * own + coefs[:, K:] * turn(own, K // 2)).astype(bf16))
            again = dot(minor[...], lanes3(mixed)).astype(bf16)
            for m in range(2):
                for g in range(G):
                    t2[g, pl.ds((2 * n + m) * R, R)] = again[
                        g * R * ZS : (g + 1) * R * ZS, m * K : (m + 1) * K
                    ].reshape(R, ZS, K)
            return carry

        lax.fori_loop(0, SPACE // 2, pair, 0, unroll=4)

        moved = dot(major[...], lanes3([t2[g].reshape(ROWS, K) for g in range(G)])).astype(bf16)
        for g in range(G):
            s2[y, g] = moved[:, g * K : (g + 1) * K].reshape(L, ZS, K)

        @pl.when(y < R - 1)
        def _():
            to_peers(
                lambda j: remote(
                    s2.at[y, :, pl.ds(j * R, R)], x2.at[:, :, sp * R + y], s2_send.at[y], x2_recv.at[y], (tm, j)
                ).start()
            )

        @pl.when(y == R - 1)
        def _():
            for g in range(G):
                to_peers(
                    lambda j: remote(
                        s2.at[y, g, pl.ds(j * R, R)], x2.at[g, :, sp * R + y], s2_send.at[y], x2_recv.at[y + g], (tm, j)
                    ).start()
                )

        x2[:, :, sp * R + y] = s2[y, :, pl.ds(sp * R, R)]

    second_coefficients()
    prod[...] = jnp.zeros_like(prod)
    for y in range(R - 1):
        arrived(x2.at[:, :, pl.ds(0, SPACE - 1)], x2_recv.at[y])

    @pl.loop(0, G)
    def _(g):
        arrived(x2.at[g, :, pl.ds(0, SPACE - 1)], x2_recv.at[R - 1 + g])
        moved = dot(major[...], lanes3([x2[g, x].reshape(ROWS, K) for x in range(R)]))
        for x in range(R):
            own = moved[:, x * K : (x + 1) * K]
            coefs = c2[g, x]
            mixed = (coefs[:, :K] * own + coefs[:, K:] * turn(own, K // 2)).astype(bf16)
            out_v[g, x] = mixed.reshape(L, ZS, K)
            target = handed.at[x, :, pl.ds(g * ZS, ZS), :]

            @pl.when(even)
            def _():
                pltpu.make_async_copy(out_v.at[g, x], target, o_recv).start()

            @pl.when(odd == 1)
            def _():
                remote(out_v.at[g, x], target, o_send, o_recv, (up, sp)).start()

        @pl.when(even)
        def _():
            products(g)

    @pl.when(odd == 1)
    def _():
        turn_trial()
        for g in range(G):
            products(g)

    total = prod[:ORB]
    for c in range(1, C4):
        total = total + turn(prod[c * ORB : (c + 1) * ORB], K - c * ORB)
    quarter = lax.broadcasted_iota(jnp.int32, (8, K), 1) // ORB
    packed = jnp.where(quarter == 0, total[:8], 0.0)
    for q in range(1, 4):
        packed = packed + jnp.where(quarter == q, turn(total[8 * q : 8 * q + 8], q * ORB), 0.0)
    p_s[...] = packed

    @pl.when(even)
    def _():
        for j in range(SPACE):
            remote(p_s, p_r.at[sp], p_sem.at[0], p_sem.at[1], (down, j)).start()
        arrived(p_r, p_sem.at[1])

    @pl.when(odd == 1)
    def _():
        p_r[sp] = packed
        to_peers(lambda j: remote(p_s, p_r.at[sp], p_sem.at[0], p_sem.at[1], (tm, j)).start())
        arrived(p_r.at[pl.ds(0, SPACE - 1)], p_sem.at[1])

    result = jnp.sum(p_r[...], axis=0) * (1.0 / math.sqrt(C4 * L**3))
    for q in range(4):
        rows = result if q == 0 else turn(result, K - q * ORB)
        projection[8 * q : 8 * q + 8, :] = rows[:, :ORB]

    arrived(fx_s, fx_sem.at[0])
    arrived(fy_s.at[pl.ds(0, SPACE - 1)], fy_sem.at[0])
    for g in range(G):
        arrived(s1.at[g, :, pl.ds(0, L - R)], s1_send.at[g])
        arrived(s2.at[g, :, pl.ds(0, L - R)], s2_send.at[g])

    @pl.when(even)
    def _():
        for g in range(G - 1):
            arrived(w_in.at[g], z_send.at[g])
        arrived(yh, f_send)
        arrived(fy_r, ff_sem.at[0])
        arrived(p_r, p_sem.at[0])

    @pl.when(odd == 1)
    def _():
        arrived(out_v, o_send)
        arrived(p_r.at[pl.ds(0, SPACE - 1)], p_sem.at[0])

    arrived(out_v, o_recv)


def body(blocks, fields, trial):
    diagonal, mats = tables()
    bf16, f32 = jnp.bfloat16, jnp.float32
    vmem = pl.BlockSpec(memory_space=pltpu.VMEM)
    hbm = pl.BlockSpec(memory_space=pl.ANY)
    dma = pltpu.SemaphoreType.DMA
    by_x = pltpu.VMEM((G, R, L, ZS, K), bf16)
    by_pair = pltpu.VMEM((G, L, R, ZS, K), bf16)
    one_row = pltpu.VMEM((G, L, ZS, K), bf16)
    packed = pltpu.VMEM((SPACE, 16, K), bf16)
    tile = pltpu.VMEM((8, K), f32)
    scratch = [pltpu.VMEM(fields.shape, f32)] + [pltpu.VMEM(m.shape, m.dtype) for m in mats]
    scratch += [
        by_x, by_x, pltpu.VMEM((L, R, ZS, K), bf16), by_pair, one_row, one_row, by_x, by_x, by_x, by_x,
        pltpu.VMEM((G, K, R * ROWS), bf16),
        pltpu.VMEM((2, R, L, K), bf16), pltpu.VMEM((2, R, L, K), bf16),
        packed, packed, packed,
        pltpu.VMEM((SPACE, R, TRI, 2 * K), f32), pltpu.VMEM((G, R, ROWS, 2 * K), f32),
        pltpu.VMEM((K, K), f32), tile, pltpu.VMEM((SPACE, 8, K), f32),
        dma((G,)), dma((G,)), dma(()), dma(()), dma((G,)), dma((G,)), dma((5,)), dma((G,)), dma((5,)), dma(()), dma(()), dma(()),
        dma((2,)), dma((2,)), dma((2,)), dma((2,)), dma((9,)),
    ]
    return pl.pallas_call(
        lambda *refs: kernel(diagonal, *refs),
        out_shape=(
            jax.ShapeDtypeStruct(blocks.shape, bf16),
            jax.ShapeDtypeStruct((ORB, ORB), f32),
        ),
        in_specs=[hbm] * (3 + len(mats)),
        out_specs=(hbm, vmem),
        scratch_shapes=scratch,
        compiler_params=pltpu.CompilerParams(
            collective_id=0, has_side_effects=True, vmem_limit_bytes=56 * 1024 * 1024
        ),
    )(blocks, fields, trial, *[jnp.asarray(m) for m in mats])


def solution(mesh):
    in_specs = (
        P(("tm", "space"), None, None, None),
        P(("tm", "space"), None, None),
        P("space", None, None, None),
    )
    out_specs = (P(("tm", "space"), None, None, None), P("tm", None))
    return jax.shard_map(body, mesh=mesh, in_specs=in_specs, out_specs=out_specs, check_vma=False)
```
